32 devices in a mesh: dp: 16 (over z, y, core), cp: 2 (over x).
Axes of the slice: x: 2, y: 2, z: 4, core: 2. Of those that a mesh axis runs over, the one named last changes fastest.
Arguments:
- tokens: bfloat16 [8192, 960], P(('dp', 'cp')), may hold values from -6 to 6
- out_grad: bfloat16 [8192, 960], P(('dp', 'cp')), may hold values from -6 to 6
- lengths: int32 [16, 3], P('dp'), may hold values from 1 to 256, 512 in all within a row
- slot_positions: int32 [16, 512], P('dp'), may hold values from 0 to 511, as said below
- params: float32 [9830400], P('cp'), as said below
- first_moment: float32 [9830400], P('cp'), as said below
- second_moment: float32 [9830400], P('cp'), as said below
- norm_gains: float32 [2, 960], P(None, 'cp'), may hold values from 0.5 to 1.5
- gain_first: float32 [2, 960], P(None, 'cp'), as said below
- gain_second: float32 [2, 960], P(None, 'cp'), as said below
Outputs:
- block_out: float32 [8192, 960], P(('dp', 'cp'))
- input_grad: float32 [8192, 960], P(('dp', 'cp'))
- param_grad: float32 [9830400], P('cp')
- new_first: float32 [9830400], P('cp')
- new_second: float32 [9830400], P('cp')
- new_params: float32 [9830400], P('cp')
- gain_grad: float32 [2, 960], P(None, 'cp')
- new_gain_first: float32 [2, 960], P(None, 'cp')
- new_gain_second: float32 [2, 960], P(None, 'cp')
- new_gains: float32 [2, 960], P(None, 'cp')
The draws below stay inside these ranges and needn't reach their ends.
Inputs may be any that keep to these rules, and one draw needn't show every extreme that they name: Each row holds the lengths of the 3 sequences of one window in the order in which they are packed; they add up to 512, and the largest is exactly 256. `slot_positions`: in each row, for every j below 256, the 2 entries c * 256 + j, for c below 2, hold the window positions j * 2 to j * 2 + 1 in some order; so each row is a permutation of the window's positions. `params`: owner blocks of the seven matrices, laid out as the steps say. `first_moment`: laid out as params. `second_moment`: laid out as params; every entry is positive. `gain_first`: one row for each norm. `gain_second`: one row for each norm; every entry is positive.
All inputs are finite; a program needn't handle non-finite values.
Results may differ from the reference program's by a relative error of at most 0.02.
Values may be sent and summed in bfloat16 or wider, within the bound.
A program may use at most 448 MiB of HBM per device.

```python
import math
import jax
import jax.numpy as jnp
import numpy as np
from jax import lax

D = 960
H = 15
KVH = 5
HD = 64
FF = 2560
TOK_DEV = 256
NSEQ = 3
STEP = 10
QD = 960
KD = 320
W = 512
MAXLEN = 256
TOKENS = 8192
N_DP = 16
N_CP = 2


def matrix_layout():
    drawn_std = D ** (-0.5)
    out_std = (MAXLEN / (6.0 * QD)) ** 0.5
    out_grad_size = (6.0 / MAXLEN) ** 0.5
    return [(D, QD, drawn_std, 1.0), (D, KD, drawn_std, 1.0), (D, KD, drawn_std, 1.0), (QD, D, out_std, out_grad_size), (D, FF, drawn_std, 0.3), (D, FF, drawn_std, 0.3), (FF, D, FF ** (-0.5), 0.5)]


def owner_scales(column_pick):
    pieces = []
    for layout_row in matrix_layout():
        pieces.append(jnp.full((layout_row[0] // N_CP * layout_row[1],), layout_row[column_pick], jnp.float32))
    return jnp.concatenate(pieces)


def draw_slot_positions(key, part):
    key = jax.random.fold_in(key, 14)
    rotation = jax.random.randint(key, (N_DP, 1, TOK_DEV), 0, N_CP, dtype=jnp.int32)
    device_ids = jnp.arange(N_CP, dtype=jnp.int32)[None, :, None]
    column_ids = jnp.arange(TOK_DEV, dtype=jnp.int32)[None, None, :]
    return (column_ids * N_CP + (device_ids - rotation) % N_CP).reshape(N_DP, W)


def draw_params(key, part):
    key = jax.random.fold_in(key, 11)
    scales = owner_scales(2)
    noise_draw = jax.random.normal(key, (N_CP, scales.shape[0]), jnp.float32)
    return (noise_draw * scales[None, :]).reshape(-1)


def draw_first_moment(key, part):
    key = jax.random.fold_in(key, 12)
    scales = owner_scales(3) * TOKENS ** 0.5 * (0.1 / 0.9)
    noise_draw = jax.random.normal(key, (N_CP, scales.shape[0]), jnp.float32)
    return (noise_draw * scales[None, :]).reshape(-1)


def draw_second_moment(key, part):
    key = jax.random.fold_in(key, 13)
    scales = owner_scales(3) ** 2 * TOKENS * (0.05 / 0.95)
    factor = jnp.exp(jax.random.uniform(key, (N_CP, scales.shape[0]), jnp.float32, 0.0, math.log(4.0)))
    return (factor * scales[None, :]).reshape(-1)


def draw_gain_first(key, part):
    key = jax.random.fold_in(key, 15)
    return jax.random.normal(key, (2, D), jnp.float32) * (0.1 / 0.9) * TOKENS ** 0.5


def draw_gain_second(key, part):
    key = jax.random.fold_in(key, 16)
    factor = jnp.exp(jax.random.uniform(key, (2, D), jnp.float32, 0.0, math.log(4.0)))
    return factor * (0.05 / 0.95) * TOKENS


def block_scale(rng, shape, split, least, largest):
    loudness = 1.0
    for dim, parts in split:
        draws = jax.random.uniform(jax.random.fold_in(jax.random.fold_in(rng, 6), dim), (parts,), jnp.float32, least / len(split), largest / len(split))
        loudness = loudness * jnp.repeat(jnp.exp(draws), shape[dim] // parts).reshape((-1,) + (1,) * (len(shape) - 1 - dim))
    return loudness


def length_profile(count, total, most, skew):
    weights = [(1 << 20) // math.isqrt(standing ** skew) + 1 for standing in range(2, count + 1)]
    surplus, holding = total - most - (count - 1), [1] * (count - 1)
    while surplus > 0:
        movable = [i for i in range(count - 1) if holding[i] < most]
        pool, budget = sum([weights[i] for i in movable]), surplus
        for i in movable:
            more = min(most - holding[i], max(1, budget * weights[i] // pool), surplus)
            holding[i] = holding[i] + more
            surplus = surplus - more
    return np.array([most] + holding)


def uneven_parts(stream_key, count, total, limit, slope):
    if count == 2:
        one = jax.random.randint(stream_key, (), max(1, total - limit), min(limit, total - 1) + 1)
        return jnp.stack([one, total - one])
    tallies = jnp.asarray(length_profile(count, total, limit, slope), jnp.int32)
    pairs = (count - 1) // 2
    giver, sink = tallies[1:1 + 2 * pairs:2], tallies[2:2 + 2 * pairs:2]
    room = jnp.minimum(giver - 1, limit - sink)
    shifted = jax.random.randint(jax.random.fold_in(stream_key, 1), (pairs,), 0, 1 << 20) % (room + 1)
    tallies = tallies.at[1:1 + 2 * pairs:2].set(giver - shifted).at[2:2 + 2 * pairs:2].set(sink + shifted)
    return tallies[jax.random.permutation(jax.random.fold_in(stream_key, 2), count)]


def centred(key, dims, scale, bound, split=(), held_as=jnp.bfloat16):
    entries = jax.random.normal(key, dims, jnp.float32) * scale
    if len(split) > 0:
        entries = block_scale(key, dims, split, -0.22, 0.18) * entries
    return jnp.clip(entries, min=-bound, max=bound).astype(held_as)


def setup_inputs(seed: int = 0) -> dict:
    arg_keys = jax.random.split(jax.random.key(seed), 11)
    tokens = centred(arg_keys[0], (TOKENS, D), 1.0, 6.0, ((0, 32),))
    out_grad = centred(arg_keys[1], (TOKENS, D), 1.0, 6.0, ((0, 32),))
    lengths = jax.vmap(lambda own: uneven_parts(own, NSEQ, W, MAXLEN, 2))(jax.random.split(arg_keys[2], N_DP)).reshape((N_DP, NSEQ)).astype(jnp.int32)
    slot_positions = draw_slot_positions(jax.random.fold_in(arg_keys[10], 71), 0)
    params = draw_params(jax.random.fold_in(arg_keys[10], 71), 0)
    first_moment = draw_first_moment(jax.random.fold_in(arg_keys[10], 71), 0)
    second_moment = draw_second_moment(jax.random.fold_in(arg_keys[10], 71), 0)
    norm_gains = jnp.clip(1.0 + 0.1 * jax.random.normal(arg_keys[7], (2, D), jnp.float32), 0.5, 1.5)
    gain_first = draw_gain_first(jax.random.fold_in(arg_keys[10], 71), 0)
    gain_second = draw_gain_second(jax.random.fold_in(arg_keys[10], 71), 0)
    return dict(tokens=tokens, out_grad=out_grad, lengths=lengths, slot_positions=slot_positions, params=params, first_moment=first_moment, second_moment=second_moment, norm_gains=norm_gains, gain_first=gain_first, gain_second=gain_second)


@jax.custom_vjp
def low(v):
    return lax.optimization_barrier(v.astype(jnp.bfloat16)).astype(jnp.float32)

@jax.custom_vjp
def low_back(v):
    return v

def low_keep(v):
    return (low(v), None)

def low_pass(kept, grad):
    return (grad,)

def back_keep(v):
    return (v, None)

def back_low(kept, grad):
    return (low(grad),)
low.defvjp(low_keep, low_pass)
low_back.defvjp(back_keep, back_low)
eps_norm = 1e-05
beta_one = 0.9
beta_two = 0.95
adam_eps = 1e-08
decay_coef = 0.1
rope_base = 10000.0
gain_rate = 1.0
masked_score = -1e+30

def matrix_shapes():
    return [(D, QD), (D, KD), (D, KD), (QD, D), (D, FF), (D, FF), (FF, D)]

def matrix_rates(longest):
    plain_rate = 3.0 * D ** (-0.5)
    out_rate = 3.0 * (longest / (6.0 * QD)) ** 0.5
    return [plain_rate, plain_rate, plain_rate, out_rate, plain_rate, plain_rate, 3.0 * FF ** (-0.5)]

def owner_rates(shard_count, longest):
    pieces = []
    for shape_pair, rate_value in zip(matrix_shapes(), matrix_rates(longest)):
        pieces.append(jnp.full((shape_pair[0] // shard_count * shape_pair[1],), rate_value, jnp.float32))
    return jnp.concatenate(pieces)

def unpack_owner(flat):
    owner_rows = flat.reshape(N_CP, -1)
    matrices = []
    offset = 0
    for row_count, col_count in matrix_shapes():
        seg_size = row_count // N_CP * col_count
        matrices.append(owner_rows[:, offset:offset + seg_size].reshape(row_count, col_count))
        offset += seg_size
    return matrices

def pack_owner(matrices):
    return jnp.concatenate([piece.reshape(N_CP, -1) for piece in matrices], axis=1).reshape(-1)

def highest(left_side, right_side):
    return jnp.dot(left_side, right_side, precision=lax.Precision.HIGHEST)

def rms_norm(values, gain_row):
    return values * lax.rsqrt(lax.optimization_barrier(jnp.mean(values * values, axis=-1, keepdims=True)) + eps_norm) * gain_row

def window_layout(seq_lengths, slot_pos):
    seq_ends = jnp.cumsum(seq_lengths).astype(jnp.int32)
    seq_starts = (seq_ends - seq_lengths).astype(jnp.int32)
    segment = lax.optimization_barrier(jnp.sum((slot_pos[:, None] >= seq_ends[None, :]).astype(jnp.int32), axis=1)).astype(jnp.int32)
    chosen = segment[:, None] == jnp.arange(seq_lengths.shape[0], dtype=jnp.int32)[None, :]
    position = (slot_pos - lax.optimization_barrier(jnp.sum(jnp.where(chosen, seq_starts[None, :], 0), axis=1))).astype(jnp.int32)
    return (segment, position)

def rope_tables(position):
    half_dim = HD // 2
    inv_freq = rope_base ** (-(jnp.arange(half_dim, dtype=jnp.float32) * 2.0 / HD))
    angles = position.astype(jnp.float32)[:, None] * inv_freq[None, :]
    return (jnp.cos(angles), jnp.sin(angles))

def rotate(values, cosine, sine_vals):
    half_dim = HD // 2
    first_half = values[..., :half_dim]
    second_half = values[..., half_dim:]
    cos_wide = cosine[:, None, :]
    sin_wide = sine_vals[:, None, :]
    return jnp.concatenate([first_half * cos_wide - second_half * sin_wide, second_half * cos_wide + first_half * sin_wide], axis=-1)

def attend(query_rot, key_rot, value_low, segment, position):
    total_rows = query_rot.shape[0]
    block_rows = min(512, total_rows)
    block_count = total_rows // block_rows
    group_size = H // KVH
    score_scale = HD ** (-0.5)
    query_blocks = query_rot.reshape(block_count, block_rows, KVH, group_size, HD)
    segment_blocks = segment.reshape(block_count, block_rows)
    position_blocks = position.reshape(block_count, block_rows)

    def one_block(block_args):
        query_blk, segment_blk, position_blk = block_args
        raw_scores = jnp.einsum('qghd,kgd->ghqk', query_blk, key_rot, precision=lax.Precision.HIGHEST)
        scores = low_back(raw_scores * score_scale)
        allowed = (segment_blk[:, None] == segment[None, :]) & (position[None, :] <= position_blk[:, None])
        scores = jnp.where(allowed[None, None], scores, masked_score)
        row_max = lax.optimization_barrier(jnp.max(scores, axis=-1, keepdims=True))
        exp_scores = jnp.exp(scores - row_max)
        probs_low = low(exp_scores / lax.optimization_barrier(jnp.sum(exp_scores, axis=-1, keepdims=True)))
        output = jnp.einsum('ghqk,kgd->qghd', probs_low, value_low, precision=lax.Precision.HIGHEST)
        return output.reshape(block_rows, H * HD)
    outputs = lax.map(jax.checkpoint(one_block), (query_blocks, segment_blocks, position_blocks))
    return outputs.reshape(total_rows, H * HD)

def window_forward(inputs, matrix_in, gains_in, segment, position):
    w_query, w_key, w_value, w_out, w_gate, w_up, w_down = [low(piece) for piece in matrix_in]
    gain_pair = low(gains_in)
    row_count = inputs.shape[0]
    xn_one = low(rms_norm(inputs, gain_pair[0]))
    cosine, sine_vals = rope_tables(position)
    query_rot = low(rotate(low_back(highest(xn_one, w_query)).reshape(row_count, H, HD), cosine, sine_vals))
    key_rot = low(rotate(low_back(highest(xn_one, w_key)).reshape(row_count, KVH, HD), cosine, sine_vals))
    value_low = low(low_back(highest(xn_one, w_value))).reshape(row_count, KVH, HD)
    attended = attend(query_rot, key_rot, value_low, segment, position)
    resid_one = inputs + low_back(highest(low(low_back(attended)), w_out))
    xn_two = low(rms_norm(resid_one, gain_pair[1]))
    gate_act = low_back(highest(xn_two, w_gate))
    up_act = low_back(highest(xn_two, w_up))
    hidden_low = low(jax.nn.silu(gate_act) * up_act)
    return resid_one + highest(hidden_low, w_down)

def adamw_step(weight, gradient, first_old, second_old, step_rates, decay_value):
    first_new = beta_one * first_old + (1.0 - beta_one) * gradient
    second_new = beta_two * second_old + (1.0 - beta_two) * gradient * gradient
    first_hat = first_new / (1.0 - beta_one ** STEP)
    second_hat = second_new / (1.0 - beta_two ** STEP)
    updated = weight - step_rates * (first_hat / (jnp.sqrt(second_hat) + adam_eps) + decay_value * weight)
    return (first_new, second_new, updated)

def reference(tokens, out_grad, lengths, slot_positions, params, first_moment, second_moment, norm_gains, gain_first, gain_second):
    matrices = unpack_owner(params)

    def one_window(summed, window_args):
        window_tokens, window_grad, seq_lengths, slot_pos = window_args
        segment, position = window_layout(seq_lengths, slot_pos)

        def forward(inputs, matrix_in, gains_in):
            return window_forward(inputs, matrix_in, gains_in, segment, position)
        output, pullback = jax.vjp(forward, window_tokens.astype(jnp.float32), matrices, norm_gains)
        input_back, matrix_back, gain_back = pullback(window_grad.astype(jnp.float32))
        summed = ([carried + fresh for carried, fresh in zip(summed[0], matrix_back)], summed[1] + gain_back)
        return (summed, (output, input_back))
    zero_grads = ([jnp.zeros_like(piece) for piece in matrices], jnp.zeros_like(norm_gains))
    windows = (tokens.reshape(N_DP, W, D), out_grad.reshape(N_DP, W, D), lengths, slot_positions)
    (matrix_grads, gain_grad), (outputs, input_backs) = lax.scan(one_window, zero_grads, windows)
    param_grad = pack_owner(matrix_grads)
    step_rates = jnp.tile(owner_rates(N_CP, MAXLEN), N_CP)
    new_first, new_second, new_params = adamw_step(params, param_grad, first_moment, second_moment, step_rates, decay_coef)
    new_gain_first, new_gain_second, new_gains = adamw_step(norm_gains, gain_grad, gain_first, gain_second, gain_rate, 0.0)
    return (outputs.reshape(TOKENS, D), input_backs.reshape(TOKENS, D), param_grad, new_first, new_second, new_params, gain_grad, new_gain_first, new_gain_second, new_gains)
```

```python
import jax
import jax.numpy as jnp
from jax import lax
from jax.sharding import PartitionSpec as P

D = 960
H = 15
KVH = 5
HD = 64
FF = 2560
STEP = 10
QD = 960
KD = 320


eps_norm = 1e-05
beta_one = 0.9
beta_two = 0.95
adam_eps = 1e-08
decay_coef = 0.1
rope_base = 10000.0
gain_rate = 1.0
masked_score = -1e30


def matrix_shapes():
    return [(D, QD), (D, KD), (D, KD), (QD, D), (D, FF), (D, FF), (FF, D)]


def matrix_rates(longest):
    plain_rate = 3.0 * D ** (-0.5)
    out_rate = 3.0 * (longest / (6.0 * QD)) ** 0.5
    return [
        plain_rate,
        plain_rate,
        plain_rate,
        out_rate,
        plain_rate,
        plain_rate,
        3.0 * FF ** (-0.5),
    ]


def owner_rates(shard_count, longest):
    pieces = []
    for shape_pair, rate_value in zip(matrix_shapes(), matrix_rates(longest)):
        pieces.append(
            jnp.full((shape_pair[0] // shard_count * shape_pair[1],), rate_value, jnp.float32)
        )
    return jnp.concatenate(pieces)


def split_owned(flat, shard_count):
    pieces = []
    offset = 0
    for row_count, col_count in matrix_shapes():
        seg_size = row_count // shard_count * col_count
        pieces.append(flat[offset : offset + seg_size].reshape(row_count // shard_count, col_count))
        offset += seg_size
    return pieces


def rms_norm(values, gain_row):
    return (
        values * lax.rsqrt(jnp.mean(values * values, axis=-1, keepdims=True) + eps_norm) * gain_row
    )


def swiglu(gate_act, up_act):
    return jax.nn.silu(gate_act) * up_act


def window_layout(seq_lengths, slot_pos):
    seq_ends = jnp.cumsum(seq_lengths)
    seq_starts = seq_ends - seq_lengths
    segment = jnp.sum((slot_pos[:, None] >= seq_ends[None, :]).astype(jnp.int32), axis=1)
    chosen = segment[:, None] == jnp.arange(seq_lengths.shape[0], dtype=jnp.int32)[None, :]
    position = slot_pos - jnp.sum(jnp.where(chosen, seq_starts[None, :], 0), axis=1)
    return (segment, position)


def rope_tables(position):
    half_dim = HD // 2
    inv_freq = rope_base ** (-(jnp.arange(half_dim, dtype=jnp.float32) * 2.0 / HD))
    angles = position.astype(jnp.float32)[:, None] * inv_freq[None, :]
    return (jnp.cos(angles), jnp.sin(angles))


def rotate(values, cosine, sine_vals, direction):
    half_dim = HD // 2
    first_half = values[..., :half_dim]
    second_half = values[..., half_dim:]
    cos_wide = cosine[:, None, :]
    sin_wide = direction * sine_vals[:, None, :]
    return jnp.concatenate(
        [
            first_half * cos_wide - second_half * sin_wide,
            second_half * cos_wide + first_half * sin_wide,
        ],
        axis=-1,
    )


def group_forward(group_args, allowed, score_scale):
    query_grp, key_grp, value_grp = group_args
    raw_scores = jnp.einsum("qhd,kd->hqk", query_grp, key_grp, preferred_element_type=jnp.float32)
    scores = jnp.where(allowed[None], raw_scores * score_scale, masked_score)
    row_max = jnp.max(scores, axis=-1, keepdims=True)
    exp_scores = jnp.exp(scores - row_max)
    row_total = jnp.sum(exp_scores, axis=-1, keepdims=True)
    probs_low = (exp_scores / row_total).astype(jnp.bfloat16)
    output = jnp.einsum("hqk,kd->qhd", probs_low, value_grp, preferred_element_type=jnp.float32)
    return (output, row_max + jnp.log(row_total))


def group_backward(group_args, allowed, score_scale):
    query_grp, key_grp, value_grp, grad_grp, log_sums = group_args
    raw_scores = jnp.einsum("qhd,kd->hqk", query_grp, key_grp, preferred_element_type=jnp.float32)
    scores = jnp.where(allowed[None], raw_scores * score_scale, masked_score)
    probs = jnp.exp(scores - log_sums)
    probs_low = probs.astype(jnp.bfloat16)
    grad_probs = jnp.einsum("qhd,kd->hqk", grad_grp, value_grp, preferred_element_type=jnp.float32)
    row_dot = jnp.sum(probs * grad_probs, axis=-1, keepdims=True)
    grad_scores = (probs * (grad_probs - row_dot)).astype(jnp.bfloat16)
    grad_query = (
        jnp.einsum("hqk,kd->qhd", grad_scores, key_grp, preferred_element_type=jnp.float32)
        * score_scale
    )
    grad_key = (
        jnp.einsum("hqk,qhd->kd", grad_scores, query_grp, preferred_element_type=jnp.float32)
        * score_scale
    )
    grad_value = jnp.einsum("hqk,qhd->kd", probs_low, grad_grp, preferred_element_type=jnp.float32)
    return (grad_query, grad_key, grad_value)


def adamw_step(weight, gradient, first_old, second_old, step_rates, decay_value):
    first_new = beta_one * first_old + (1.0 - beta_one) * gradient
    second_new = beta_two * second_old + (1.0 - beta_two) * gradient * gradient
    first_hat = first_new / (1.0 - beta_one**STEP)
    second_hat = second_new / (1.0 - beta_two**STEP)
    updated = weight - step_rates * (
        first_hat / (jnp.sqrt(second_hat) + adam_eps) + decay_value * weight
    )
    return (first_new, second_new, updated)


def swap_shards(values):
    return lax.ppermute(values, "cp", [(0, 1), (1, 0)])


def swap_replicas(values, distance):
    return lax.ppermute(
        values, "dp", [(index, index ^ distance) for index in range(lax.axis_size("dp"))]
    )


def in_order(mine, theirs, my_shard, axis):
    return jnp.where(
        my_shard == 0,
        jnp.concatenate([mine, theirs], axis=axis),
        jnp.concatenate([theirs, mine], axis=axis),
    )


def split_columns(values, my_shard):
    half = values.shape[1] // 2
    lower, upper = values[:, :half], values[:, half:]
    return (jnp.where(my_shard == 0, lower, upper), jnp.where(my_shard == 0, upper, lower))


def gather_rows(half):
    my_shard = lax.axis_index("cp")
    quarter = lax.axis_index("dp") % 4
    mine = half.reshape(4, half.shape[0] // 4, half.shape[1])
    other = (1 - my_shard) * 4
    fetched = swap_shards(lax.dynamic_index_in_dim(mine, quarter, 0))
    across = swap_replicas(fetched, 2)
    whole = jnp.zeros((8,) + mine.shape[1:], half.dtype)
    whole = lax.dynamic_update_slice_in_dim(whole, mine, my_shard * 4, 0)
    for piece, place in (
        (fetched, quarter),
        (across, quarter ^ 2),
        (swap_replicas(fetched, 1), quarter ^ 1),
        (swap_replicas(across, 1), quarter ^ 3),
    ):
        whole = lax.dynamic_update_slice_in_dim(whole, piece, other + place, 0)
    return whole.reshape(-1, half.shape[1])


def owned_product(left_mine, left_peer, right_mine, right_peer):
    left = jnp.concatenate([left_mine, left_peer], axis=0)
    right = jnp.concatenate([right_mine, right_peer], axis=0)
    return jnp.dot(left.T, right, preferred_element_type=jnp.float32).astype(jnp.bfloat16)


def scatter_replicas(matrices):
    flat = jnp.concatenate([piece.reshape(-1, 128) for piece in matrices], axis=0)
    return lax.psum_scatter(flat, "dp", scatter_dimension=0, tiled=True)


def body(
    tokens,
    out_grad,
    lengths,
    slot_positions,
    params,
    first_moment,
    second_moment,
    norm_gains,
    gain_first,
    gain_second,
):
    low_type = jnp.bfloat16
    shard_count = lax.axis_size("cp")
    replica_count = lax.axis_size("dp")
    local_rows = tokens.shape[0]
    longest = local_rows * shard_count // 2
    group_size = H // KVH
    score_scale = HD ** (-0.5)
    my_shard = lax.axis_index("cp")
    low_params = params.astype(low_type)
    half_query, half_key, half_value, half_out, half_gate, half_up, half_down = split_owned(
        low_params, shard_count
    )
    gains_low = norm_gains.astype(low_type)
    gain_pair = in_order(gains_low, swap_shards(gains_low), my_shard, 1)
    w_qkv = gather_rows(jnp.concatenate([half_query, half_key, half_value], axis=1))
    w_out = gather_rows(half_out)
    w_pair = gather_rows(jnp.concatenate([half_gate, half_up], axis=1))
    w_down = gather_rows(half_down)

    out_peer = swap_shards(out_grad)
    segment_all, position_all = window_layout(lengths[0], slot_positions[0])

    def shard_rows(values, shard):
        return lax.dynamic_slice_in_dim(values, shard * local_rows, local_rows)

    segment_mine = shard_rows(segment_all, my_shard)
    position_mine = shard_rows(position_all, my_shard)
    segment_keys = jnp.concatenate([segment_mine, shard_rows(segment_all, 1 - my_shard)])
    position_keys = jnp.concatenate([position_mine, shard_rows(position_all, 1 - my_shard)])
    allowed = (segment_mine[:, None] == segment_keys[None, :]) & (
        position_keys[None, :] <= position_mine[:, None]
    )
    cosine, sine_vals = rope_tables(position_mine)
    inputs = tokens.astype(jnp.float32)
    normed_one, pull_one = jax.vjp(rms_norm, inputs, gain_pair[0].astype(jnp.float32))
    xn_one = normed_one.astype(low_type)
    one_mine, one_theirs = split_columns(xn_one, my_shard)
    one_peer = swap_shards(one_theirs)
    qkv_pre = jnp.dot(xn_one, w_qkv, preferred_element_type=jnp.float32)
    query_pre = qkv_pre[:, :QD]
    key_pre = qkv_pre[:, QD : QD + KD]
    value_low = qkv_pre[:, QD + KD :].astype(low_type)
    query_rot = rotate(query_pre.reshape(local_rows, H, HD), cosine, sine_vals, 1.0).astype(
        low_type
    )
    key_rot = rotate(key_pre.reshape(local_rows, KVH, HD), cosine, sine_vals, 1.0).astype(low_type)
    key_value = jnp.concatenate([key_rot.reshape(local_rows, KD), value_low], axis=1)
    key_value = jnp.concatenate([key_value, swap_shards(key_value)], axis=0)
    key_groups = key_value[:, :KD].reshape(-1, KVH, HD).transpose(1, 0, 2)
    value_groups = key_value[:, KD:].reshape(-1, KVH, HD).transpose(1, 0, 2)
    query_groups = query_rot.reshape(local_rows, KVH, group_size, HD).transpose(1, 0, 2, 3)
    attended, log_sums = lax.map(
        lambda group_args: group_forward(group_args, allowed, score_scale),
        (query_groups, key_groups, value_groups),
    )
    attn_low = attended.transpose(1, 0, 2, 3).reshape(local_rows, QD).astype(low_type)
    attn_mine, attn_theirs = split_columns(attn_low, my_shard)
    attn_peer = swap_shards(attn_theirs)
    resid_one = inputs + jnp.dot(attn_low, w_out, preferred_element_type=jnp.float32)
    normed_two, pull_two = jax.vjp(rms_norm, resid_one, gain_pair[1].astype(jnp.float32))
    xn_two = normed_two.astype(low_type)
    two_mine, two_theirs = split_columns(xn_two, my_shard)
    two_peer = swap_shards(two_theirs)
    pair_act = jnp.dot(xn_two, w_pair, preferred_element_type=jnp.float32)
    gate_act = pair_act[:, :FF]
    up_act = pair_act[:, FF:]
    hidden_act, pull_act = jax.vjp(swiglu, gate_act, up_act)
    hidden_low = hidden_act.astype(low_type)
    hidden_mine, hidden_theirs = split_columns(hidden_low, my_shard)
    hidden_peer = swap_shards(hidden_theirs)
    block_out = resid_one + jnp.dot(hidden_low, w_down, preferred_element_type=jnp.float32)
    grad_hidden = jnp.dot(out_grad, w_down.T, preferred_element_type=jnp.float32)
    grad_gate_act, grad_up_act = pull_act(grad_hidden)
    pair_back = jnp.concatenate(
        [grad_gate_act.astype(low_type), grad_up_act.astype(low_type)], axis=1
    )
    pair_peer = swap_shards(pair_back)
    grad_down = owned_product(hidden_mine, hidden_peer, out_grad, out_peer)
    down_piece = scatter_replicas([grad_down])
    grad_xn_two = jnp.dot(pair_back, w_pair.T, preferred_element_type=jnp.float32)
    back_two, gain_grad_two = pull_two(grad_xn_two)
    grad_resid = out_grad.astype(jnp.float32) + back_two
    resid_low = grad_resid.astype(low_type)
    resid_peer = swap_shards(resid_low)
    grad_pair = owned_product(two_mine, two_peer, pair_back, pair_peer)
    pair_piece = scatter_replicas([grad_pair[:, :FF], grad_pair[:, FF:]])
    grad_attn = jnp.dot(resid_low, w_out.T, preferred_element_type=jnp.float32).astype(low_type)
    grad_groups = grad_attn.reshape(local_rows, KVH, group_size, HD).transpose(1, 0, 2, 3)
    grad_q, grad_k_part, grad_v_part = lax.map(
        lambda group_args: group_backward(group_args, allowed, score_scale),
        (query_groups, key_groups, value_groups, grad_groups, log_sums),
    )
    key_terms = grad_k_part.transpose(1, 0, 2).reshape(-1, KD)
    value_terms = grad_v_part.transpose(1, 0, 2).reshape(-1, KD)
    terms = jnp.concatenate([key_terms, value_terms], axis=1)
    terms_mine = terms[:local_rows] + swap_shards(terms[local_rows:].astype(low_type)).astype(
        jnp.float32
    )
    query_back = rotate(
        grad_q.transpose(1, 0, 2, 3).reshape(local_rows, H, HD), cosine, sine_vals, -1.0
    )
    key_back = rotate(terms_mine[:, :KD].reshape(local_rows, KVH, HD), cosine, sine_vals, -1.0)
    qkv_back = jnp.concatenate(
        [
            query_back.reshape(local_rows, QD).astype(low_type),
            key_back.reshape(local_rows, KD).astype(low_type),
            terms_mine[:, KD:].astype(low_type),
        ],
        axis=1,
    )
    qkv_peer = swap_shards(qkv_back)
    grad_xn_one = jnp.dot(qkv_back, w_qkv.T, preferred_element_type=jnp.float32)
    back_one, gain_grad_one = pull_one(grad_xn_one)
    input_grad = grad_resid + back_one
    grad_out = owned_product(attn_mine, attn_peer, resid_low, resid_peer)
    grad_qkv = owned_product(one_mine, one_peer, qkv_back, qkv_peer)
    attn_piece = scatter_replicas(
        [grad_qkv[:, :QD], grad_qkv[:, QD : QD + KD], grad_qkv[:, QD + KD :], grad_out]
    )
    gain_all = lax.psum(jnp.stack([gain_grad_one, gain_grad_two]), ("dp", "cp"))
    gain_owned = split_columns(gain_all, my_shard)[0]
    owned_grad = jnp.concatenate(
        [
            lax.all_gather(piece, "dp", axis=0, tiled=True).reshape(-1)
            for piece in (attn_piece, pair_piece, down_piece)
        ]
    ).astype(jnp.float32)
    step_rates = owner_rates(shard_count, longest)
    new_first, new_second, new_params = adamw_step(
        params, owned_grad, first_moment, second_moment, step_rates, decay_coef
    )
    new_gain_first, new_gain_second, new_gains = adamw_step(
        norm_gains, gain_owned, gain_first, gain_second, gain_rate, 0.0
    )
    return (
        block_out,
        input_grad,
        owned_grad,
        new_first,
        new_second,
        new_params,
        gain_owned,
        new_gain_first,
        new_gain_second,
        new_gains,
    )


def solution(mesh):
    return jax.shard_map(
        body,
        mesh=mesh,
        in_specs=(
            P(("dp", "cp"), None),
            P(("dp", "cp"), None),
            P("dp", None),
            P("dp", None),
            P("cp"),
            P("cp"),
            P("cp"),
            P(None, "cp"),
            P(None, "cp"),
            P(None, "cp"),
        ),
        out_specs=(
            P(("dp", "cp"), None),
            P(("dp", "cp"), None),
            P("cp"),
            P("cp"),
            P("cp"),
            P("cp"),
            P(None, "cp"),
            P(None, "cp"),
            P(None, "cp"),
            P(None, "cp"),
        ),
        check_vma=False,
    )
```

```python
import jax
import jax.numpy as jnp
from jax import lax
from jax.experimental import pallas as pl
from jax.experimental.pallas import tpu as pltpu
from jax.sharding import PartitionSpec as P

D = 960
H = 15
KVH = 5
HD = 64
FF = 2560
STEP = 10
QD = 960
KD = 320


eps_norm = 1e-05
beta_one = 0.9
beta_two = 0.95
adam_eps = 1e-08
decay_coef = 0.1
rope_base = 10000.0
gain_rate = 1.0
masked_score = -1e30


def matrix_shapes():
    return [(D, QD), (D, KD), (D, KD), (QD, D), (D, FF), (D, FF), (FF, D)]


def matrix_rates(longest):
    plain_rate = 3.0 * D ** (-0.5)
    out_rate = 3.0 * (longest / (6.0 * QD)) ** 0.5
    return [
        plain_rate,
        plain_rate,
        plain_rate,
        out_rate,
        plain_rate,
        plain_rate,
        3.0 * FF ** (-0.5),
    ]


def rms_norm(values, gain_row):
    return (
        values * lax.rsqrt(jnp.mean(values * values, axis=-1, keepdims=True) + eps_norm) * gain_row
    )


def swiglu(gate_act, up_act):
    return jax.nn.silu(gate_act) * up_act


def window_layout(seq_lengths, slot_pos):
    seq_ends = jnp.cumsum(seq_lengths)
    seq_starts = seq_ends - seq_lengths
    segment = jnp.sum((slot_pos[:, None] >= seq_ends[None, :]).astype(jnp.int32), axis=1)
    chosen = segment[:, None] == jnp.arange(seq_lengths.shape[0], dtype=jnp.int32)[None, :]
    position = slot_pos - jnp.sum(jnp.where(chosen, seq_starts[None, :], 0), axis=1)
    return (segment, position)


def rope_tables(position):
    half_dim = HD // 2
    inv_freq = rope_base ** (-(jnp.arange(half_dim, dtype=jnp.float32) * 2.0 / HD))
    angles = position.astype(jnp.float32)[:, None] * inv_freq[None, :]
    return (jnp.cos(angles), jnp.sin(angles))


def rotate(values, cosine, sine_vals, direction):
    half_dim = HD // 2
    first_half = values[..., :half_dim]
    second_half = values[..., half_dim:]
    cos_wide = cosine[:, None, :]
    sin_wide = direction * sine_vals[:, None, :]
    return jnp.concatenate(
        [
            first_half * cos_wide - second_half * sin_wide,
            second_half * cos_wide + first_half * sin_wide,
        ],
        axis=-1,
    )


def group_forward(group_args, allowed, score_scale):
    query_grp, key_grp, value_grp = group_args
    raw_scores = jnp.einsum("qhd,kd->hqk", query_grp, key_grp, preferred_element_type=jnp.float32)
    scores = jnp.where(allowed[None], raw_scores * score_scale, masked_score)
    row_max = jnp.max(scores, axis=-1, keepdims=True)
    exp_scores = jnp.exp(scores - row_max)
    row_total = jnp.sum(exp_scores, axis=-1, keepdims=True)
    probs_low = (exp_scores / row_total).astype(jnp.bfloat16)
    output = jnp.einsum("hqk,kd->qhd", probs_low, value_grp, preferred_element_type=jnp.float32)
    return (output, row_max + jnp.log(row_total))


def group_backward(group_args, allowed, score_scale):
    query_grp, key_grp, value_grp, grad_grp, log_sums = group_args
    raw_scores = jnp.einsum("qhd,kd->hqk", query_grp, key_grp, preferred_element_type=jnp.float32)
    scores = jnp.where(allowed[None], raw_scores * score_scale, masked_score)
    probs = jnp.exp(scores - log_sums)
    probs_low = probs.astype(jnp.bfloat16)
    grad_probs = jnp.einsum("qhd,kd->hqk", grad_grp, value_grp, preferred_element_type=jnp.float32)
    row_dot = jnp.sum(probs * grad_probs, axis=-1, keepdims=True)
    grad_scores = (probs * (grad_probs - row_dot)).astype(jnp.bfloat16)
    grad_query = (
        jnp.einsum("hqk,kd->qhd", grad_scores, key_grp, preferred_element_type=jnp.float32)
        * score_scale
    )
    grad_key = (
        jnp.einsum("hqk,qhd->kd", grad_scores, query_grp, preferred_element_type=jnp.float32)
        * score_scale
    )
    grad_value = jnp.einsum("hqk,qhd->kd", probs_low, grad_grp, preferred_element_type=jnp.float32)
    return (grad_query, grad_key, grad_value)


def adamw_step(weight, gradient, first_old, second_old, step_rates, decay_value):
    first_new = beta_one * first_old + (1.0 - beta_one) * gradient
    second_new = beta_two * second_old + (1.0 - beta_two) * gradient * gradient
    first_hat = first_new / (1.0 - beta_one**STEP)
    second_hat = second_new / (1.0 - beta_two**STEP)
    updated = weight - step_rates * (
        first_hat / (jnp.sqrt(second_hat) + adam_eps) + decay_value * weight
    )
    return (first_new, second_new, updated)


def swap_shards(values):
    return lax.ppermute(values, "cp", [(0, 1), (1, 0)])


def swap_replicas(values, distance):
    return lax.ppermute(
        values, "dp", [(index, index ^ distance) for index in range(lax.axis_size("dp"))]
    )


def in_order(mine, theirs, my_shard, axis):
    return jnp.where(
        my_shard == 0,
        jnp.concatenate([mine, theirs], axis=axis),
        jnp.concatenate([theirs, mine], axis=axis),
    )


def split_columns(values, my_shard):
    half = values.shape[1] // 2
    lower, upper = values[:, :half], values[:, half:]
    return (jnp.where(my_shard == 0, lower, upper), jnp.where(my_shard == 0, upper, lower))


def gather_rows(params, columns):
    my_shard = lax.axis_index("cp")
    quarter = lax.axis_index("dp") % 4
    low_type = jnp.bfloat16

    def piece_of(start, size):
        return lax.dynamic_slice_in_dim(params, start, size).astype(low_type)

    fetched = jnp.concatenate(
        [
            piece_of(offset + quarter * (rows // 4 * width), rows // 4 * width).reshape(
                1, rows // 4, width
            )
            for offset, rows, width in columns
        ],
        axis=2,
    )
    fetched = swap_shards(fetched)
    mine = jnp.concatenate(
        [
            params[offset : offset + rows * width].astype(low_type).reshape(4, rows // 4, width)
            for offset, rows, width in columns
        ],
        axis=2,
    )
    across = swap_replicas(fetched, 2)
    whole = jnp.concatenate([mine, mine], axis=0)
    other = (1 - my_shard) * 4
    for piece, place in (
        (fetched, quarter),
        (across, quarter ^ 2),
        (swap_replicas(fetched, 1), quarter ^ 1),
        (swap_replicas(across, 1), quarter ^ 3),
    ):
        whole = lax.dynamic_update_slice_in_dim(whole, piece, other + place, 0)
    return whole.reshape(-1, whole.shape[2])


def owned_product(left_mine, left_peer, right_mine, right_peer):
    left = jnp.concatenate([left_mine, left_peer], axis=0)
    right = jnp.concatenate([right_mine, right_peer], axis=0)
    return jnp.dot(left.T, right, preferred_element_type=jnp.float32).astype(jnp.bfloat16)


def scatter_replicas(flat, distance):
    bit = (lax.axis_index("dp") // distance) % 2
    halves = flat.reshape(2, flat.shape[0] // 2, flat.shape[1])
    mine = lax.dynamic_index_in_dim(halves, bit, 0, keepdims=False)
    theirs = lax.dynamic_index_in_dim(halves, 1 - bit, 0, keepdims=False)
    received = swap_replicas(theirs, distance)
    return (mine.astype(jnp.float32) + received.astype(jnp.float32)).astype(jnp.bfloat16)


def scatter_steps(flat, distance, limit):
    while distance < limit:
        flat = scatter_replicas(flat, distance)
        distance *= 2
    return flat


def gather_steps(piece):
    distance = lax.axis_size("dp") // 2
    while distance >= 1:
        bit = (lax.axis_index("dp") // distance) % 2
        piece = in_order(piece, swap_replicas(piece, distance), bit, 0)
        distance //= 2
    return piece


BLOCK = 1200
CHUNK_BLOCKS = 8


def update_kernel(first_rate, last_rate, split, *refs):
    params_ref, first_ref, second_ref, grad_ref = refs[:4]
    grad_out, first_out, second_out, params_out = refs[-4:]
    gradient = grad_ref[...].astype(jnp.float32)
    rate = jnp.where(pl.program_id(0) < split, first_rate, last_rate)
    grad_out[...] = gradient
    first_out[...], second_out[...], params_out[...] = adamw_step(
        params_ref[...], gradient, first_ref[...], second_ref[...], rate, decay_coef
    )


def update_chunk(state, gradient, chunk, rates, split, earlier):
    rows = state[0].shape[0]

    def state_block(i):
        return (chunk * CHUNK_BLOCKS + i, 0)

    spec = pl.BlockSpec((BLOCK, 128), state_block)
    grad_spec = pl.BlockSpec((BLOCK, 128), lambda i: (i, 0))
    return pl.pallas_call(
        lambda *refs: update_kernel(rates[0], rates[1], split, *refs),
        grid=(CHUNK_BLOCKS,),
        in_specs=[spec] * 3 + [grad_spec] + [pl.BlockSpec(memory_space=pl.ANY)] * len(earlier),
        out_specs=[spec] * 4,
        out_shape=[jax.ShapeDtypeStruct((rows, 128), jnp.float32)] * 4,
        input_output_aliases={4 + index: index for index in range(len(earlier))},
        compiler_params=pltpu.CompilerParams(vmem_limit_bytes=40 * 1024 * 1024),
        cost_estimate=pl.CostEstimate(
            flops=20 * BLOCK * CHUNK_BLOCKS * 128,
            bytes_accessed=30 * BLOCK * CHUNK_BLOCKS * 128,
            transcendentals=0,
        ),
    )(*state, gradient, *earlier)


def body(
    tokens,
    out_grad,
    lengths,
    slot_positions,
    params,
    first_moment,
    second_moment,
    norm_gains,
    gain_first,
    gain_second,
):
    low_type = jnp.bfloat16
    shard_count = lax.axis_size("cp")
    replica_count = lax.axis_size("dp")
    local_rows = tokens.shape[0]
    longest = local_rows * shard_count // 2
    group_size = H // KVH
    score_scale = HD ** (-0.5)
    my_shard = lax.axis_index("cp")
    blocks = []
    offset = 0
    for row_count, col_count in matrix_shapes():
        blocks.append((offset, row_count // shard_count, col_count))
        offset += row_count // shard_count * col_count
    gains_low = norm_gains.astype(low_type)
    gain_pair = in_order(gains_low, swap_shards(gains_low), my_shard, 1)
    w_qkv = gather_rows(params, blocks[:3])
    w_out = gather_rows(params, blocks[3:4])
    w_pair = gather_rows(params, blocks[4:6])
    w_down = gather_rows(params, blocks[6:])

    out_peer = swap_shards(out_grad)
    segment_all, position_all = window_layout(lengths[0], slot_positions[0])

    def shard_rows(values, shard):
        return lax.dynamic_slice_in_dim(values, shard * local_rows, local_rows)

    segment_mine = shard_rows(segment_all, my_shard)
    position_mine = shard_rows(position_all, my_shard)
    segment_keys = jnp.concatenate([segment_mine, shard_rows(segment_all, 1 - my_shard)])
    position_keys = jnp.concatenate([position_mine, shard_rows(position_all, 1 - my_shard)])
    allowed = (segment_mine[:, None] == segment_keys[None, :]) & (
        position_keys[None, :] <= position_mine[:, None]
    )
    cosine, sine_vals = rope_tables(position_mine)
    inputs = tokens.astype(jnp.float32)
    normed_one, pull_one = jax.vjp(rms_norm, inputs, gain_pair[0].astype(jnp.float32))
    xn_one = normed_one.astype(low_type)
    one_mine, one_theirs = split_columns(xn_one, my_shard)
    one_peer = swap_shards(one_theirs)
    qkv_pre = jnp.dot(xn_one, w_qkv, preferred_element_type=jnp.float32)
    query_pre = qkv_pre[:, :QD]
    key_pre = qkv_pre[:, QD : QD + KD]
    value_low = qkv_pre[:, QD + KD :].astype(low_type)
    query_rot = rotate(query_pre.reshape(local_rows, H, HD), cosine, sine_vals, 1.0).astype(
        low_type
    )
    key_rot = rotate(key_pre.reshape(local_rows, KVH, HD), cosine, sine_vals, 1.0).astype(low_type)
    key_value = jnp.concatenate([key_rot.reshape(local_rows, KD), value_low], axis=1)
    key_value = jnp.concatenate([key_value, swap_shards(key_value)], axis=0)
    key_groups = key_value[:, :KD].reshape(-1, KVH, HD).transpose(1, 0, 2)
    value_groups = key_value[:, KD:].reshape(-1, KVH, HD).transpose(1, 0, 2)
    query_groups = query_rot.reshape(local_rows, KVH, group_size, HD).transpose(1, 0, 2, 3)
    forward_groups = [
        group_forward(
            (query_groups[group], key_groups[group], value_groups[group]), allowed, score_scale
        )
        for group in range(KVH)
    ]
    attn_low = jnp.concatenate(
        [attended.reshape(local_rows, -1).astype(low_type) for attended, _ in forward_groups],
        axis=1,
    )
    attn_low, one_peer, out_peer = lax.optimization_barrier((attn_low, one_peer, out_peer))
    attn_mine, attn_theirs = split_columns(attn_low, my_shard)
    attn_peer = swap_shards(attn_theirs)
    resid_one = inputs + jnp.dot(attn_low, w_out, preferred_element_type=jnp.float32)
    normed_two, pull_two = jax.vjp(rms_norm, resid_one, gain_pair[1].astype(jnp.float32))
    xn_two = normed_two.astype(low_type)
    two_mine, two_theirs = split_columns(xn_two, my_shard)
    two_peer = swap_shards(two_theirs)
    pair_act = jnp.dot(xn_two, w_pair, preferred_element_type=jnp.float32)
    gate_act = pair_act[:, :FF]
    up_act = pair_act[:, FF:]
    hidden_act, pull_act = jax.vjp(swiglu, gate_act, up_act)
    hidden_low = hidden_act.astype(low_type)
    hidden_mine, hidden_theirs = split_columns(hidden_low, my_shard)
    hidden_peer = swap_shards(hidden_theirs)
    block_out = resid_one + jnp.dot(hidden_low, w_down, preferred_element_type=jnp.float32)
    grad_hidden = jnp.dot(out_grad, w_down.T, preferred_element_type=jnp.float32)
    grad_gate_act, grad_up_act = pull_act(grad_hidden)
    gate_back = grad_gate_act.astype(low_type)
    up_back = grad_up_act.astype(low_type)
    gate_peer = swap_shards(gate_back)
    up_peer = swap_shards(up_back)
    pair_back = jnp.concatenate([gate_back, up_back], axis=1)
    pair_back, attn_peer, two_peer = lax.optimization_barrier((pair_back, attn_peer, two_peer))
    grad_xn_two = jnp.dot(pair_back, w_pair.T, preferred_element_type=jnp.float32)
    back_two, gain_grad_two = pull_two(grad_xn_two)
    grad_resid = out_grad.astype(jnp.float32) + back_two
    resid_low = grad_resid.astype(low_type)
    resid_low, hidden_peer = lax.optimization_barrier((resid_low, hidden_peer))
    resid_peer = swap_shards(resid_low)
    grad_down = owned_product(hidden_mine, hidden_peer, out_grad, out_peer).reshape(-1, 128)
    down_part = scatter_replicas(grad_down, 1)
    grad_attn = jnp.dot(resid_low, w_out.T, preferred_element_type=jnp.float32).astype(low_type)
    grad_groups = grad_attn.reshape(local_rows, KVH, group_size, HD).transpose(1, 0, 2, 3)
    backward_groups = []
    for group in range(KVH):
        grad_group = grad_groups[group]
        if group == 3:
            grad_group, down_part = lax.optimization_barrier((grad_group, down_part))
            down_part = scatter_replicas(down_part, 2)
        backward_groups.append(
            group_backward(
                (
                    query_groups[group],
                    key_groups[group],
                    value_groups[group],
                    grad_group,
                    forward_groups[group][1],
                ),
                allowed,
                score_scale,
            )
        )
    grad_q = jnp.stack([terms[0] for terms in backward_groups], axis=1)
    key_terms = jnp.concatenate([terms[1] for terms in backward_groups], axis=1)
    value_terms = jnp.concatenate([terms[2] for terms in backward_groups], axis=1)
    terms = jnp.concatenate([key_terms, value_terms], axis=1)
    terms, gate_peer, down_part = lax.optimization_barrier((terms, gate_peer, down_part))
    grad_gate = owned_product(two_mine, two_peer, gate_back, gate_peer).reshape(-1, 128)
    gate_part = scatter_replicas(grad_gate, 1)
    terms_mine = terms[:local_rows] + swap_shards(terms[local_rows:].astype(low_type)).astype(
        jnp.float32
    )
    query_back = rotate(
        grad_q.reshape(local_rows, H, HD), cosine, sine_vals, -1.0
    )
    key_back = rotate(terms_mine[:, :KD].reshape(local_rows, KVH, HD), cosine, sine_vals, -1.0)
    qkv_back = jnp.concatenate(
        [
            query_back.reshape(local_rows, QD).astype(low_type),
            key_back.reshape(local_rows, KD).astype(low_type),
            terms_mine[:, KD:].astype(low_type),
        ],
        axis=1,
    )
    qkv_back, up_peer, gate_part = lax.optimization_barrier((qkv_back, up_peer, gate_part))
    grad_up = owned_product(two_mine, two_peer, up_back, up_peer).reshape(-1, 128)
    qkv_peer = swap_shards(qkv_back)
    grad_xn_one = jnp.dot(qkv_back, w_qkv.T, preferred_element_type=jnp.float32)
    back_one, gain_grad_one = pull_one(grad_xn_one)
    input_grad = grad_resid + back_one
    grad_out = owned_product(attn_mine, attn_peer, resid_low, resid_peer)
    grad_qkv = owned_product(one_mine, one_peer, qkv_back, qkv_peer)
    gain_local = jnp.stack([gain_grad_one, gain_grad_two])
    gain_mine, gain_theirs = split_columns(gain_local, my_shard)
    gain_rows = (gain_mine + swap_shards(gain_theirs)).astype(low_type).reshape(-1)
    gain_rows = jnp.pad(gain_rows, (0, 128 * 128 - gain_rows.shape[0])).reshape(128, 128)
    grad_attn_owned = jnp.concatenate(
        [
            grad_qkv[:, :QD].reshape(-1, 128),
            grad_qkv[:, QD : QD + KD].reshape(-1, 128),
            grad_qkv[:, QD + KD :].reshape(-1, 128),
            grad_out.reshape(-1, 128),
            gain_rows,
        ],
        axis=0,
    )
    down_sum = gather_steps(scatter_steps(down_part, 4, replica_count))
    gate_sum = gather_steps(scatter_steps(gate_part, 2, replica_count))
    up_sum = gather_steps(scatter_steps(grad_up, 1, replica_count))
    attn_sum = gather_steps(scatter_steps(grad_attn_owned, 1, replica_count))
    gain_owned = attn_sum[9600:9608].reshape(-1)[: 2 * (D // shard_count)]
    gain_owned = gain_owned.reshape(2, -1).astype(jnp.float32)
    rates = matrix_rates(longest)
    state = [values.reshape(-1, 128) for values in (params, first_moment, second_moment)]
    updated = update_chunk(state, down_sum, 3, (rates[6], rates[6]), 0, ())
    updated = update_chunk(state, gate_sum, 1, (rates[4], rates[4]), 0, updated)
    updated = update_chunk(state, up_sum, 2, (rates[5], rates[5]), 0, updated)
    updated = update_chunk(state, attn_sum, 0, (rates[0], rates[3]), 5, updated)
    owned_grad, new_first, new_second, new_params = [values.reshape(-1) for values in updated]
    new_gain_first, new_gain_second, new_gains = adamw_step(
        norm_gains, gain_owned, gain_first, gain_second, gain_rate, 0.0
    )
    return (
        block_out,
        input_grad,
        owned_grad,
        new_first,
        new_second,
        new_params,
        gain_owned,
        new_gain_first,
        new_gain_second,
        new_gains,
    )


def solution(mesh):
    return jax.shard_map(
        body,
        mesh=mesh,
        in_specs=(
            P(("dp", "cp"), None),
            P(("dp", "cp"), None),
            P("dp", None),
            P("dp", None),
            P("cp"),
            P("cp"),
            P("cp"),
            P(None, "cp"),
            P(None, "cp"),
            P(None, "cp"),
        ),
        out_specs=(
            P(("dp", "cp"), None),
            P(("dp", "cp"), None),
            P("cp"),
            P("cp"),
            P("cp"),
            P("cp"),
            P(None, "cp"),
            P(None, "cp"),
            P(None, "cp"),
            P(None, "cp"),
        ),
        check_vma=False,
    )
```

```python
import jax
import jax.numpy as jnp
from jax import lax
from jax.experimental import pallas as pl
from jax.experimental.pallas import tpu as pltpu
from jax.sharding import PartitionSpec as P

D = 960
H = 15
KVH = 5
HD = 64
FF = 2560
STEP = 10
QD = 960
KD = 320


eps_norm = 1e-05
beta_one = 0.9
beta_two = 0.95
adam_eps = 1e-08
decay_coef = 0.1
rope_base = 10000.0
gain_rate = 1.0
masked_score = -1e30


def matrix_shapes():
    return [(D, QD), (D, KD), (D, KD), (QD, D), (D, FF), (D, FF), (FF, D)]


def matrix_rates(longest):
    plain_rate = 3.0 * D ** (-0.5)
    out_rate = 3.0 * (longest / (6.0 * QD)) ** 0.5
    return [
        plain_rate,
        plain_rate,
        plain_rate,
        out_rate,
        plain_rate,
        plain_rate,
        3.0 * FF ** (-0.5),
    ]


def rms_norm(values, gain_row):
    return (
        values * lax.rsqrt(jnp.mean(values * values, axis=-1, keepdims=True) + eps_norm) * gain_row
    )


def swiglu(gate_act, up_act):
    return jax.nn.silu(gate_act) * up_act


def window_layout(seq_lengths, slot_pos):
    seq_ends = jnp.cumsum(seq_lengths)
    seq_starts = seq_ends - seq_lengths
    segment = jnp.sum((slot_pos[:, None] >= seq_ends[None, :]).astype(jnp.int32), axis=1)
    chosen = segment[:, None] == jnp.arange(seq_lengths.shape[0], dtype=jnp.int32)[None, :]
    position = slot_pos - jnp.sum(jnp.where(chosen, seq_starts[None, :], 0), axis=1)
    return (segment, position)


def rope_tables(position):
    half_dim = HD // 2
    inv_freq = rope_base ** (-(jnp.arange(half_dim, dtype=jnp.float32) * 2.0 / HD))
    angles = position.astype(jnp.float32)[:, None] * inv_freq[None, :]
    return (jnp.cos(angles), jnp.sin(angles))


def rotate(values, cosine, sine_vals, direction):
    half_dim = HD // 2
    first_half = values[..., :half_dim]
    second_half = values[..., half_dim:]
    cos_wide = cosine[:, None, :]
    sin_wide = direction * sine_vals[:, None, :]
    return jnp.concatenate(
        [
            first_half * cos_wide - second_half * sin_wide,
            second_half * cos_wide + first_half * sin_wide,
        ],
        axis=-1,
    )


def group_forward(group_args, allowed, score_scale):
    query_grp, key_grp, value_grp = group_args
    raw_scores = jnp.einsum("qhd,kd->hqk", query_grp, key_grp, preferred_element_type=jnp.float32)
    scores = jnp.where(allowed[None], raw_scores * score_scale, masked_score)
    row_max = jnp.max(scores, axis=-1, keepdims=True)
    exp_scores = jnp.exp(scores - row_max)
    row_total = jnp.sum(exp_scores, axis=-1, keepdims=True)
    probs_low = (exp_scores / row_total).astype(jnp.bfloat16)
    output = jnp.einsum("hqk,kd->qhd", probs_low, value_grp, preferred_element_type=jnp.float32)
    return (output, row_max + jnp.log(row_total))


def group_backward(group_args, allowed, score_scale):
    query_grp, key_grp, value_grp, grad_grp, log_sums = group_args
    raw_scores = jnp.einsum("qhd,kd->hqk", query_grp, key_grp, preferred_element_type=jnp.float32)
    scores = jnp.where(allowed[None], raw_scores * score_scale, masked_score)
    probs = jnp.exp(scores - log_sums)
    probs_low = probs.astype(jnp.bfloat16)
    grad_probs = jnp.einsum("qhd,kd->hqk", grad_grp, value_grp, preferred_element_type=jnp.float32)
    row_dot = jnp.sum(probs * grad_probs, axis=-1, keepdims=True)
    grad_scores = (probs * (grad_probs - row_dot)).astype(jnp.bfloat16)
    grad_query = (
        jnp.einsum("hqk,kd->qhd", grad_scores, key_grp, preferred_element_type=jnp.float32)
        * score_scale
    )
    grad_key = (
        jnp.einsum("hqk,qhd->kd", grad_scores, query_grp, preferred_element_type=jnp.float32)
        * score_scale
    )
    grad_value = jnp.einsum("hqk,qhd->kd", probs_low, grad_grp, preferred_element_type=jnp.float32)
    return (grad_query, grad_key, grad_value)


def adamw_step(weight, gradient, first_old, second_old, step_rates, decay_value):
    first_new = beta_one * first_old + (1.0 - beta_one) * gradient
    second_new = beta_two * second_old + (1.0 - beta_two) * gradient * gradient
    first_hat = first_new / (1.0 - beta_one**STEP)
    second_hat = second_new / (1.0 - beta_two**STEP)
    updated = weight - step_rates * (
        first_hat / (jnp.sqrt(second_hat) + adam_eps) + decay_value * weight
    )
    return (first_new, second_new, updated)


def swap_shards(values):
    return lax.ppermute(values, "cp", [(0, 1), (1, 0)])


def swap_replicas(values, distance):
    return lax.ppermute(
        values, "dp", [(index, index ^ distance) for index in range(lax.axis_size("dp"))]
    )


def in_order(mine, theirs, my_shard, axis):
    return jnp.where(
        my_shard == 0,
        jnp.concatenate([mine, theirs], axis=axis),
        jnp.concatenate([theirs, mine], axis=axis),
    )


def split_columns(values, my_shard):
    half = values.shape[1] // 2
    lower, upper = values[:, :half], values[:, half:]
    return (jnp.where(my_shard == 0, lower, upper), jnp.where(my_shard == 0, upper, lower))


def fetch_quarter(params, columns):
    quarter = lax.axis_index("dp") % 4
    pieces = [
        lax.dynamic_slice_in_dim(
            params, offset + quarter * (rows // 4 * width), rows // 4 * width
        )
        .astype(jnp.bfloat16)
        .reshape(1, rows // 4, width)
        for offset, rows, width in columns
    ]
    return swap_shards(jnp.concatenate(pieces, axis=2))


def gather_rows(params, columns, fetched):
    my_shard = lax.axis_index("cp")
    quarter = lax.axis_index("dp") % 4
    across = swap_replicas(fetched, 2)
    mine = jnp.concatenate(
        [
            params[offset : offset + rows * width]
            .astype(jnp.bfloat16)
            .reshape(4, rows // 4, width)
            for offset, rows, width in columns
        ],
        axis=2,
    )
    whole = jnp.concatenate([mine, mine], axis=0)
    other = (1 - my_shard) * 4
    for piece, place in (
        (fetched, quarter),
        (across, quarter ^ 2),
        (swap_replicas(fetched, 1), quarter ^ 1),
        (swap_replicas(across, 1), quarter ^ 3),
    ):
        whole = lax.dynamic_update_slice_in_dim(whole, piece, other + place, 0)
    return whole.reshape(-1, whole.shape[2])


def owned_product(left_mine, left_peer, right_mine, right_peer):
    left = jnp.concatenate([left_mine, left_peer], axis=0)
    right = jnp.concatenate([right_mine, right_peer], axis=0)
    return jnp.dot(left.T, right, preferred_element_type=jnp.float32).astype(jnp.bfloat16)


def scatter_replicas(flat, distance):
    bit = (lax.axis_index("dp") // distance) % 2
    halves = flat.reshape(2, flat.shape[0] // 2, flat.shape[1])
    mine = lax.dynamic_index_in_dim(halves, bit, 0, keepdims=False)
    theirs = lax.dynamic_index_in_dim(halves, 1 - bit, 0, keepdims=False)
    received = swap_replicas(theirs, distance)
    return (mine.astype(jnp.float32) + received.astype(jnp.float32)).astype(jnp.bfloat16)


def scatter_steps(flat, distance, limit):
    while distance < limit:
        flat = scatter_replicas(flat, distance)
        distance *= 2
    return flat


def gather_steps(piece):
    distance = lax.axis_size("dp") // 2
    while distance >= 2:
        bit = (lax.axis_index("dp") // distance) % 2
        piece = in_order(piece, swap_replicas(piece, distance), bit, 0)
        distance //= 2
    return (piece, swap_replicas(piece, 1))


BLOCK = 1200
CHUNK_BLOCKS = 8


def update_kernel(first_rate, last_rate, split, bit_ref, *refs):
    params_ref, first_ref, second_ref, mine_ref, received_ref = refs[:5]
    grad_out, first_out, second_out, params_out = refs[-4:]
    own_half = pl.program_id(0) // (CHUNK_BLOCKS // 2) == bit_ref[0]
    gradient = jnp.where(
        own_half, mine_ref[...].astype(jnp.float32), received_ref[...].astype(jnp.float32)
    )
    rate = jnp.where(pl.program_id(0) < split, first_rate, last_rate)
    grad_out[...] = gradient
    first_out[...], second_out[...], params_out[...] = adamw_step(
        params_ref[...], gradient, first_ref[...], second_ref[...], rate, decay_coef
    )


def update_chunk(state, halves, bit, chunk, rates, split, earlier):
    rows = state[0].shape[0]

    def state_block(i):
        return (chunk * CHUNK_BLOCKS + i, 0)

    spec = pl.BlockSpec((BLOCK, 128), state_block)
    half_spec = pl.BlockSpec((BLOCK, 128), lambda i: (i % (CHUNK_BLOCKS // 2), 0))
    return pl.pallas_call(
        lambda *refs: update_kernel(rates[0], rates[1], split, *refs),
        grid=(CHUNK_BLOCKS,),
        in_specs=[pl.BlockSpec(memory_space=pltpu.SMEM)]
        + [spec] * 3
        + [half_spec] * 2
        + [pl.BlockSpec(memory_space=pl.ANY)] * len(earlier),
        out_specs=[spec] * 4,
        out_shape=[jax.ShapeDtypeStruct((rows, 128), jnp.float32)] * 4,
        input_output_aliases={6 + index: index for index in range(len(earlier))},
        compiler_params=pltpu.CompilerParams(vmem_limit_bytes=40 * 1024 * 1024),
        cost_estimate=pl.CostEstimate(
            flops=20 * BLOCK * CHUNK_BLOCKS * 128,
            bytes_accessed=32 * BLOCK * CHUNK_BLOCKS * 128,
            transcendentals=0,
        ),
    )(bit, *state, *halves, *earlier)


def body(
    tokens,
    out_grad,
    lengths,
    slot_positions,
    params,
    first_moment,
    second_moment,
    norm_gains,
    gain_first,
    gain_second,
):
    low_type = jnp.bfloat16
    shard_count = lax.axis_size("cp")
    replica_count = lax.axis_size("dp")
    local_rows = tokens.shape[0]
    longest = local_rows * shard_count // 2
    group_size = H // KVH
    score_scale = HD ** (-0.5)
    my_shard = lax.axis_index("cp")
    blocks = []
    offset = 0
    for row_count, col_count in matrix_shapes():
        blocks.append((offset, row_count // shard_count, col_count))
        offset += row_count // shard_count * col_count
    gains_low = norm_gains.astype(low_type)
    gain_pair = in_order(gains_low, swap_shards(gains_low), my_shard, 1)
    fetched = [
        fetch_quarter(params, columns)
        for columns in (blocks[:3], blocks[3:4], blocks[4:6], blocks[6:])
    ]
    w_qkv = gather_rows(params, blocks[:3], fetched[0])
    held, fetched[0] = lax.optimization_barrier((params, fetched[0]))
    w_out = gather_rows(held, blocks[3:4], fetched[1])
    held, fetched[1] = lax.optimization_barrier((held, fetched[1]))
    w_pair = gather_rows(held, blocks[4:6], fetched[2])
    held, fetched[2] = lax.optimization_barrier((held, fetched[2]))
    w_down = gather_rows(held, blocks[6:], fetched[3])

    out_peer = swap_shards(out_grad)
    segment_all, position_all = window_layout(lengths[0], slot_positions[0])

    def shard_rows(values, shard):
        return lax.dynamic_slice_in_dim(values, shard * local_rows, local_rows)

    segment_mine = shard_rows(segment_all, my_shard)
    position_mine = shard_rows(position_all, my_shard)
    segment_keys = jnp.concatenate([segment_mine, shard_rows(segment_all, 1 - my_shard)])
    position_keys = jnp.concatenate([position_mine, shard_rows(position_all, 1 - my_shard)])
    allowed = (segment_mine[:, None] == segment_keys[None, :]) & (
        position_keys[None, :] <= position_mine[:, None]
    )
    cosine, sine_vals = rope_tables(position_mine)
    inputs = tokens.astype(jnp.float32)
    normed_one, pull_one = jax.vjp(rms_norm, inputs, gain_pair[0].astype(jnp.float32))
    xn_one = normed_one.astype(low_type)
    one_mine, one_theirs = split_columns(xn_one, my_shard)
    one_peer = swap_shards(one_theirs)
    qkv_pre = jnp.dot(xn_one, w_qkv, preferred_element_type=jnp.float32)
    query_pre = qkv_pre[:, :QD]
    key_pre = qkv_pre[:, QD : QD + KD]
    value_low = qkv_pre[:, QD + KD :].astype(low_type)
    query_rot = rotate(query_pre.reshape(local_rows, H, HD), cosine, sine_vals, 1.0).astype(
        low_type
    )
    key_rot = rotate(key_pre.reshape(local_rows, KVH, HD), cosine, sine_vals, 1.0).astype(low_type)
    key_value = jnp.concatenate([key_rot.reshape(local_rows, KD), value_low], axis=1)
    key_value = jnp.concatenate([key_value, swap_shards(key_value)], axis=0)
    key_groups = key_value[:, :KD].reshape(-1, KVH, HD).transpose(1, 0, 2)
    value_groups = key_value[:, KD:].reshape(-1, KVH, HD).transpose(1, 0, 2)
    query_groups = query_rot.reshape(local_rows, KVH, group_size, HD).transpose(1, 0, 2, 3)
    forward_groups = [
        group_forward(
            (query_groups[group], key_groups[group], value_groups[group]), allowed, score_scale
        )
        for group in range(KVH)
    ]
    attn_low = jnp.concatenate(
        [attended.reshape(local_rows, -1).astype(low_type) for attended, _ in forward_groups],
        axis=1,
    )
    attn_low, one_peer, out_peer = lax.optimization_barrier((attn_low, one_peer, out_peer))
    attn_mine, attn_theirs = split_columns(attn_low, my_shard)
    attn_peer = swap_shards(attn_theirs)
    resid_one = inputs + jnp.dot(attn_low, w_out, preferred_element_type=jnp.float32)
    normed_two, pull_two = jax.vjp(rms_norm, resid_one, gain_pair[1].astype(jnp.float32))
    xn_two = normed_two.astype(low_type)
    two_mine, two_theirs = split_columns(xn_two, my_shard)
    two_peer = swap_shards(two_theirs)
    pair_act = jnp.dot(xn_two, w_pair, preferred_element_type=jnp.float32)
    gate_act = pair_act[:, :FF]
    up_act = pair_act[:, FF:]
    hidden_act, pull_act = jax.vjp(swiglu, gate_act, up_act)
    hidden_low = hidden_act.astype(low_type)
    hidden_mine, hidden_theirs = split_columns(hidden_low, my_shard)
    hidden_peer = swap_shards(hidden_theirs)
    block_out = resid_one + jnp.dot(hidden_low, w_down, preferred_element_type=jnp.float32)
    grad_hidden = jnp.dot(out_grad, w_down.T, preferred_element_type=jnp.float32)
    grad_gate_act, grad_up_act = pull_act(grad_hidden)
    gate_back = grad_gate_act.astype(low_type)
    up_back = grad_up_act.astype(low_type)
    pair_back = jnp.concatenate([gate_back, up_back], axis=1)
    pair_back, attn_peer, two_peer = lax.optimization_barrier((pair_back, attn_peer, two_peer))
    grad_xn_two = jnp.dot(pair_back, w_pair.T, preferred_element_type=jnp.float32)
    gate_sent, hidden_peer, grad_xn_two = lax.optimization_barrier(
        (gate_back, hidden_peer, grad_xn_two)
    )
    gate_peer = swap_shards(gate_sent)
    back_two, gain_grad_two = pull_two(grad_xn_two)
    grad_resid = out_grad.astype(jnp.float32) + back_two
    resid_low = grad_resid.astype(low_type)
    resid_peer = swap_shards(resid_low)
    grad_down = owned_product(hidden_mine, hidden_peer, out_grad, out_peer).reshape(-1, 128)
    down_part = scatter_replicas(grad_down, 1)
    grad_attn = jnp.dot(resid_low, w_out.T, preferred_element_type=jnp.float32).astype(low_type)
    grad_groups = grad_attn.reshape(local_rows, KVH, group_size, HD).transpose(1, 0, 2, 3)
    backward_groups = []
    for group in range(KVH):
        grad_group = grad_groups[group]
        if group == 3:
            earlier_group = backward_groups[2]
            grad_group, down_part, earlier_group = lax.optimization_barrier(
                (grad_group, down_part, earlier_group)
            )
            backward_groups[2] = earlier_group
            down_part = scatter_replicas(down_part, 2)
            up_sent, gate_peer, grad_group = lax.optimization_barrier(
                (up_back, gate_peer, grad_group)
            )
            up_peer = swap_shards(up_sent)
        backward_groups.append(
            group_backward(
                (
                    query_groups[group],
                    key_groups[group],
                    value_groups[group],
                    grad_group,
                    forward_groups[group][1],
                ),
                allowed,
                score_scale,
            )
        )
    grad_q = jnp.stack([terms[0] for terms in backward_groups], axis=1)
    key_terms = jnp.concatenate([terms[1] for terms in backward_groups], axis=1)
    value_terms = jnp.concatenate([terms[2] for terms in backward_groups], axis=1)
    terms = jnp.concatenate([key_terms, value_terms], axis=1)
    terms, gate_peer, down_part = lax.optimization_barrier((terms, gate_peer, down_part))
    grad_gate = owned_product(two_mine, two_peer, gate_back, gate_peer).reshape(-1, 128)
    gate_part = scatter_replicas(grad_gate, 1)
    terms_mine = terms[:local_rows] + swap_shards(terms[local_rows:].astype(low_type)).astype(
        jnp.float32
    )
    query_back = rotate(
        grad_q.reshape(local_rows, H, HD), cosine, sine_vals, -1.0
    )
    key_back = rotate(terms_mine[:, :KD].reshape(local_rows, KVH, HD), cosine, sine_vals, -1.0)
    qkv_back = jnp.concatenate(
        [
            query_back.reshape(local_rows, QD).astype(low_type),
            key_back.reshape(local_rows, KD).astype(low_type),
            terms_mine[:, KD:].astype(low_type),
        ],
        axis=1,
    )
    qkv_back, up_peer, gate_part = lax.optimization_barrier((qkv_back, up_peer, gate_part))
    grad_up = owned_product(two_mine, two_peer, up_back, up_peer).reshape(-1, 128)
    qkv_peer = swap_shards(qkv_back)
    grad_xn_one = jnp.dot(qkv_back, w_qkv.T, preferred_element_type=jnp.float32)
    back_one, gain_grad_one = pull_one(grad_xn_one)
    input_grad = grad_resid + back_one
    grad_out = owned_product(attn_mine, attn_peer, resid_low, resid_peer)
    grad_qkv = owned_product(one_mine, one_peer, qkv_back, qkv_peer)
    gain_local = jnp.stack([gain_grad_one, gain_grad_two])
    gain_mine, gain_theirs = split_columns(gain_local, my_shard)
    gain_rows = (gain_mine + swap_shards(gain_theirs)).astype(low_type).reshape(-1)
    gain_rows = jnp.pad(gain_rows, (0, 128 * 128 - gain_rows.shape[0])).reshape(128, 128)
    half_rows = BLOCK * CHUNK_BLOCKS // 2
    key_rows = grad_qkv[:, QD : QD + KD].reshape(-1, 128)
    grad_attn_owned = jnp.concatenate(
        [
            grad_qkv[:, :QD].reshape(-1, 128),
            key_rows,
            gain_rows[:64],
            grad_qkv[:, QD + KD :].reshape(-1, 128),
            grad_out.reshape(-1, 128),
            gain_rows[64:],
        ],
        axis=0,
    )
    down_sum = gather_steps(scatter_steps(down_part, 4, replica_count))
    gate_sum = gather_steps(scatter_steps(gate_part, 2, replica_count))
    up_sum = gather_steps(scatter_steps(grad_up, 1, replica_count))
    attn_sum = gather_steps(scatter_steps(grad_attn_owned, 1, replica_count))
    core = lax.axis_index("dp") % 2
    gain_sum = jnp.where(core == 0, attn_sum[0][half_rows:], attn_sum[1][half_rows:])
    gain_owned = gain_sum[:8].reshape(-1)[: 2 * (D // shard_count)]
    gain_owned = gain_owned.reshape(2, -1).astype(jnp.float32)
    rates = matrix_rates(longest)
    bit = core.reshape(1).astype(jnp.int32)
    state = [values.reshape(-1, 128) for values in (params, first_moment, second_moment)]
    updated = update_chunk(state, down_sum, bit, 3, (rates[6], rates[6]), 0, ())
    updated = update_chunk(state, gate_sum, bit, 1, (rates[4], rates[4]), 0, updated)
    updated = update_chunk(state, up_sum, bit, 2, (rates[5], rates[5]), 0, updated)
    updated = update_chunk(state, attn_sum, bit, 0, (rates[0], rates[3]), 5, updated)
    owned_grad, new_first, new_second, new_params = [values.reshape(-1) for values in updated]
    new_gain_first, new_gain_second, new_gains = adamw_step(
        norm_gains, gain_owned, gain_first, gain_second, gain_rate, 0.0
    )
    return (
        block_out,
        input_grad,
        owned_grad,
        new_first,
        new_second,
        new_params,
        gain_owned,
        new_gain_first,
        new_gain_second,
        new_gains,
    )


def solution(mesh):
    return jax.shard_map(
        body,
        mesh=mesh,
        in_specs=(
            P(("dp", "cp"), None),
            P(("dp", "cp"), None),
            P("dp", None),
            P("dp", None),
            P("cp"),
            P("cp"),
            P("cp"),
            P(None, "cp"),
            P(None, "cp"),
            P(None, "cp"),
        ),
        out_specs=(
            P(("dp", "cp"), None),
            P(("dp", "cp"), None),
            P("cp"),
            P("cp"),
            P("cp"),
            P("cp"),
            P(None, "cp"),
            P(None, "cp"),
            P(None, "cp"),
            P(None, "cp"),
        ),
        check_vma=False,
    )
```

```python
import jax
import jax.numpy as jnp
from jax import lax
from jax.experimental import pallas as pl
from jax.experimental.pallas import tpu as pltpu
from jax.sharding import PartitionSpec as P

D = 960
H = 15
KVH = 5
HD = 64
FF = 2560
STEP = 10
QD = 960
KD = 320


eps_norm = 1e-05
beta_one = 0.9
beta_two = 0.95
adam_eps = 1e-08
decay_coef = 0.1
rope_base = 10000.0
gain_rate = 1.0
masked_score = -1e30


def matrix_shapes():
    return [(D, QD), (D, KD), (D, KD), (QD, D), (D, FF), (D, FF), (FF, D)]


def matrix_rates(longest):
    plain_rate = 3.0 * D ** (-0.5)
    out_rate = 3.0 * (longest / (6.0 * QD)) ** 0.5
    return [
        plain_rate,
        plain_rate,
        plain_rate,
        out_rate,
        plain_rate,
        plain_rate,
        3.0 * FF ** (-0.5),
    ]


def rms_norm(values, gain_row):
    return (
        values * lax.rsqrt(jnp.mean(values * values, axis=-1, keepdims=True) + eps_norm) * gain_row
    )


def swiglu(gate_act, up_act):
    return jax.nn.silu(gate_act) * up_act


def window_layout(seq_lengths, slot_pos):
    seq_ends = jnp.cumsum(seq_lengths)
    seq_starts = seq_ends - seq_lengths
    segment = jnp.sum((slot_pos[:, None] >= seq_ends[None, :]).astype(jnp.int32), axis=1)
    chosen = segment[:, None] == jnp.arange(seq_lengths.shape[0], dtype=jnp.int32)[None, :]
    position = slot_pos - jnp.sum(jnp.where(chosen, seq_starts[None, :], 0), axis=1)
    return (segment, position)


def rope_tables(position):
    half_dim = HD // 2
    inv_freq = rope_base ** (-(jnp.arange(half_dim, dtype=jnp.float32) * 2.0 / HD))
    angles = position.astype(jnp.float32)[:, None] * inv_freq[None, :]
    return (jnp.cos(angles), jnp.sin(angles))


def rotate(values, cosine, sine_vals, direction):
    half_dim = HD // 2
    first_half = values[..., :half_dim]
    second_half = values[..., half_dim:]
    cos_wide = cosine[:, None, :]
    sin_wide = direction * sine_vals[:, None, :]
    return jnp.concatenate(
        [
            first_half * cos_wide - second_half * sin_wide,
            second_half * cos_wide + first_half * sin_wide,
        ],
        axis=-1,
    )


def group_forward(group_args, allowed, score_scale):
    query_grp, key_grp, value_grp = group_args
    raw_scores = jnp.einsum("qhd,kd->hqk", query_grp, key_grp, preferred_element_type=jnp.float32)
    scores = jnp.where(allowed[None], raw_scores * score_scale, masked_score)
    row_max = jnp.max(scores, axis=-1, keepdims=True)
    exp_scores = jnp.exp(scores - row_max)
    row_total = jnp.sum(exp_scores, axis=-1, keepdims=True)
    probs_low = (exp_scores / row_total).astype(jnp.bfloat16)
    output = jnp.einsum("hqk,kd->qhd", probs_low, value_grp, preferred_element_type=jnp.float32)
    return (output, row_max + jnp.log(row_total))


def group_backward(group_args, allowed, score_scale):
    query_grp, key_grp, value_grp, grad_grp, log_sums = group_args
    raw_scores = jnp.einsum("qhd,kd->hqk", query_grp, key_grp, preferred_element_type=jnp.float32)
    scores = jnp.where(allowed[None], raw_scores * score_scale, masked_score)
    probs = jnp.exp(scores - log_sums)
    probs_low = probs.astype(jnp.bfloat16)
    grad_probs = jnp.einsum("qhd,kd->hqk", grad_grp, value_grp, preferred_element_type=jnp.float32)
    row_dot = jnp.sum(probs * grad_probs, axis=-1, keepdims=True)
    grad_scores = (probs * (grad_probs - row_dot)).astype(jnp.bfloat16)
    grad_query = (
        jnp.einsum("hqk,kd->qhd", grad_scores, key_grp, preferred_element_type=jnp.float32)
        * score_scale
    )
    grad_key = (
        jnp.einsum("hqk,qhd->kd", grad_scores, query_grp, preferred_element_type=jnp.float32)
        * score_scale
    )
    grad_value = jnp.einsum("hqk,qhd->kd", probs_low, grad_grp, preferred_element_type=jnp.float32)
    return (grad_query, grad_key, grad_value)


def adamw_step(weight, gradient, first_old, second_old, step_rates, decay_value):
    first_new = beta_one * first_old + (1.0 - beta_one) * gradient
    second_new = beta_two * second_old + (1.0 - beta_two) * gradient * gradient
    first_hat = first_new / (1.0 - beta_one**STEP)
    second_hat = second_new / (1.0 - beta_two**STEP)
    updated = weight - step_rates * (
        first_hat / (jnp.sqrt(second_hat) + adam_eps) + decay_value * weight
    )
    return (first_new, second_new, updated)


def swap_shards(values):
    return lax.ppermute(values, "cp", [(0, 1), (1, 0)])


def swap_replicas(values, distance):
    return lax.ppermute(
        values, "dp", [(index, index ^ distance) for index in range(lax.axis_size("dp"))]
    )


def in_order(mine, theirs, my_shard, axis):
    return jnp.where(
        my_shard == 0,
        jnp.concatenate([mine, theirs], axis=axis),
        jnp.concatenate([theirs, mine], axis=axis),
    )


def split_columns(values, my_shard):
    half = values.shape[1] // 2
    lower, upper = values[:, :half], values[:, half:]
    return (jnp.where(my_shard == 0, lower, upper), jnp.where(my_shard == 0, upper, lower))


def fetch_quarter(params, columns):
    quarter = lax.axis_index("dp") % 4
    pieces = [
        lax.dynamic_slice_in_dim(
            params, offset + quarter * (rows // 4 * width), rows // 4 * width
        )
        .astype(jnp.bfloat16)
        .reshape(1, rows // 4, width)
        for offset, rows, width in columns
    ]
    return swap_shards(jnp.concatenate(pieces, axis=2))


def own_rows(params, columns):
    offset, rows, width = columns
    return (
        params[offset : offset + rows * width].astype(jnp.bfloat16).reshape(4, rows // 4, width)
    )


def gather_rows(mine, fetched, across):
    quarter = lax.axis_index("dp") % 4
    mine = jnp.concatenate(mine, axis=2)
    whole = jnp.concatenate([mine, mine], axis=0)
    other = (1 - lax.axis_index("cp")) * 4
    for piece, place in (
        (fetched, quarter),
        (across, quarter ^ 2),
        (swap_replicas(fetched, 1), quarter ^ 1),
        (swap_replicas(across, 1), quarter ^ 3),
    ):
        whole = lax.dynamic_update_slice_in_dim(whole, piece, other + place, 0)
    return whole.reshape(-1, whole.shape[2])


def owned_product(left_mine, left_peer, right_mine, right_peer):
    left = jnp.concatenate([left_mine, left_peer], axis=0)
    right = jnp.concatenate([right_mine, right_peer], axis=0)
    return jnp.dot(left.T, right, preferred_element_type=jnp.float32).astype(jnp.bfloat16)


def scatter_replicas(flat, distance):
    bit = (lax.axis_index("dp") // distance) % 2
    halves = flat.reshape(2, flat.shape[0] // 2, flat.shape[1])
    mine = lax.dynamic_index_in_dim(halves, bit, 0, keepdims=False)
    theirs = lax.dynamic_index_in_dim(halves, 1 - bit, 0, keepdims=False)
    received = swap_replicas(theirs, distance)
    return (mine.astype(jnp.float32) + received.astype(jnp.float32)).astype(jnp.bfloat16)


def scatter_steps(flat, distance, limit):
    while distance < limit:
        flat = scatter_replicas(flat, distance)
        distance *= 2
    return flat


def gather_steps(piece, distance, last):
    while distance >= last:
        bit = (lax.axis_index("dp") // distance) % 2
        piece = in_order(piece, swap_replicas(piece, distance), bit, 0)
        distance //= 2
    return piece


def gather_halves(part):
    piece = gather_steps(part, lax.axis_size("dp") // 2, 2)
    return (piece, swap_replicas(piece, 1))


BLOCK = 1200
CHUNK_BLOCKS = 8


def update_kernel(first_rate, last_rate, split, bit_ref, *refs):
    params_ref, first_ref, second_ref, mine_ref, received_ref = refs[:5]
    grad_out, first_out, second_out, params_out, mark_out = refs[-5:]
    mark_out[...] = jnp.zeros_like(mark_out)
    own_half = pl.program_id(0) // (CHUNK_BLOCKS // 2) == bit_ref[0]
    gradient = jnp.where(
        own_half, mine_ref[...].astype(jnp.float32), received_ref[...].astype(jnp.float32)
    )
    rate = jnp.where(pl.program_id(0) < split, first_rate, last_rate)
    grad_out[...] = gradient
    first_out[...], second_out[...], params_out[...] = adamw_step(
        params_ref[...], gradient, first_ref[...], second_ref[...], rate, decay_coef
    )


def update_chunk(state, halves, bit, chunk, rates, split, earlier):
    rows = state[0].shape[0]

    def state_block(i):
        return (chunk * CHUNK_BLOCKS + i, 0)

    spec = pl.BlockSpec((BLOCK, 128), state_block)
    half_spec = pl.BlockSpec((BLOCK, 128), lambda i: (i % (CHUNK_BLOCKS // 2), 0))
    return pl.pallas_call(
        lambda *refs: update_kernel(rates[0], rates[1], split, *refs),
        grid=(CHUNK_BLOCKS,),
        in_specs=[pl.BlockSpec(memory_space=pltpu.SMEM)]
        + [spec] * 3
        + [half_spec] * 2
        + [pl.BlockSpec(memory_space=pl.ANY)] * len(earlier),
        out_specs=[spec] * 4 + [pl.BlockSpec((8, 128), lambda i: (0, 0))],
        out_shape=[jax.ShapeDtypeStruct((rows, 128), jnp.float32)] * 4
        + [jax.ShapeDtypeStruct((8, 128), jnp.float32)],
        input_output_aliases={6 + index: index for index in range(len(earlier))},
        compiler_params=pltpu.CompilerParams(vmem_limit_bytes=40 * 1024 * 1024),
        cost_estimate=pl.CostEstimate(
            flops=20 * BLOCK * CHUNK_BLOCKS * 128,
            bytes_accessed=32 * BLOCK * CHUNK_BLOCKS * 128,
            transcendentals=0,
        ),
    )(bit, *state, *halves, *earlier)


def body(
    tokens,
    out_grad,
    lengths,
    slot_positions,
    params,
    first_moment,
    second_moment,
    norm_gains,
    gain_first,
    gain_second,
):
    low_type = jnp.bfloat16
    shard_count = lax.axis_size("cp")
    replica_count = lax.axis_size("dp")
    local_rows = tokens.shape[0]
    longest = local_rows * shard_count // 2
    group_size = H // KVH
    score_scale = HD ** (-0.5)
    my_shard = lax.axis_index("cp")
    blocks = []
    offset = 0
    for row_count, col_count in matrix_shapes():
        blocks.append((offset, row_count // shard_count, col_count))
        offset += row_count // shard_count * col_count
    gains_low = norm_gains.astype(low_type)
    gain_pair = in_order(gains_low, swap_shards(gains_low), my_shard, 1)
    fetched = [
        fetch_quarter(params, columns)
        for columns in (blocks[:3], blocks[3:4], blocks[4:6], blocks[6:])
    ]
    own_qkv = [own_rows(params, columns) for columns in blocks[:3]]
    own_out = own_rows(params, blocks[3])
    held, fetched[0], fetched[1], fetched[2] = lax.optimization_barrier(
        (params, fetched[0], fetched[1], fetched[2])
    )
    across = [swap_replicas(piece, 2) for piece in fetched]
    own_gate = own_rows(held, blocks[4])
    held, across[0], across[1], across[2] = lax.optimization_barrier(
        (held, across[0], across[1], across[2])
    )
    own_up = own_rows(held, blocks[5])
    own_down = own_rows(held, blocks[6])
    w_qkv = gather_rows(own_qkv, fetched[0], across[0])
    w_out = gather_rows([own_out], fetched[1], across[1])
    w_pair = gather_rows([own_gate, own_up], fetched[2], across[2])
    w_down = gather_rows([own_down], fetched[3], across[3])

    out_peer = swap_shards(out_grad)
    segment_all, position_all = window_layout(lengths[0], slot_positions[0])

    def shard_rows(values, shard):
        return lax.dynamic_slice_in_dim(values, shard * local_rows, local_rows)

    segment_mine = shard_rows(segment_all, my_shard)
    position_mine = shard_rows(position_all, my_shard)
    segment_keys = jnp.concatenate([segment_mine, shard_rows(segment_all, 1 - my_shard)])
    position_keys = jnp.concatenate([position_mine, shard_rows(position_all, 1 - my_shard)])
    allowed = (segment_mine[:, None] == segment_keys[None, :]) & (
        position_keys[None, :] <= position_mine[:, None]
    )
    cosine, sine_vals = rope_tables(position_mine)
    inputs = tokens.astype(jnp.float32)
    normed_one, pull_one = jax.vjp(rms_norm, inputs, gain_pair[0].astype(jnp.float32))
    xn_one = normed_one.astype(low_type)
    one_mine, one_theirs = split_columns(xn_one, my_shard)
    one_peer = swap_shards(one_theirs)
    qkv_pre = jnp.dot(xn_one, w_qkv, preferred_element_type=jnp.float32)
    query_pre = qkv_pre[:, :QD]
    key_pre = qkv_pre[:, QD : QD + KD]
    value_low = qkv_pre[:, QD + KD :].astype(low_type)
    query_rot = rotate(query_pre.reshape(local_rows, H, HD), cosine, sine_vals, 1.0).astype(
        low_type
    )
    key_rot = rotate(key_pre.reshape(local_rows, KVH, HD), cosine, sine_vals, 1.0).astype(low_type)
    key_value = jnp.concatenate([key_rot.reshape(local_rows, KD), value_low], axis=1)
    key_value = jnp.concatenate([key_value, swap_shards(key_value)], axis=0)
    key_groups = key_value[:, :KD].reshape(-1, KVH, HD).transpose(1, 0, 2)
    value_groups = key_value[:, KD:].reshape(-1, KVH, HD).transpose(1, 0, 2)
    query_groups = query_rot.reshape(local_rows, KVH, group_size, HD).transpose(1, 0, 2, 3)
    forward_groups = [
        group_forward(
            (query_groups[group], key_groups[group], value_groups[group]), allowed, score_scale
        )
        for group in range(KVH)
    ]
    attn_low = jnp.concatenate(
        [attended.reshape(local_rows, -1).astype(low_type) for attended, _ in forward_groups],
        axis=1,
    )
    attn_low, one_peer, out_peer = lax.optimization_barrier((attn_low, one_peer, out_peer))
    attn_mine, attn_theirs = split_columns(attn_low, my_shard)
    attn_peer = swap_shards(attn_theirs)
    resid_one = inputs + jnp.dot(attn_low, w_out, preferred_element_type=jnp.float32)
    normed_two, pull_two = jax.vjp(rms_norm, resid_one, gain_pair[1].astype(jnp.float32))
    xn_two = normed_two.astype(low_type)
    two_mine, two_theirs = split_columns(xn_two, my_shard)
    two_peer = swap_shards(two_theirs)
    pair_act = jnp.dot(xn_two, w_pair, preferred_element_type=jnp.float32)
    gate_act = pair_act[:, :FF]
    up_act = pair_act[:, FF:]
    hidden_act, pull_act = jax.vjp(swiglu, gate_act, up_act)
    hidden_low = hidden_act.astype(low_type)
    hidden_mine, hidden_theirs = split_columns(hidden_low, my_shard)
    hidden_peer = swap_shards(hidden_theirs)
    block_out = resid_one + jnp.dot(hidden_low, w_down, preferred_element_type=jnp.float32)
    grad_hidden = jnp.dot(out_grad, w_down.T, preferred_element_type=jnp.float32)
    grad_gate_act, grad_up_act = pull_act(grad_hidden)
    gate_back = grad_gate_act.astype(low_type)
    up_back = grad_up_act.astype(low_type)
    gate_peer = swap_shards(gate_back)
    up_peer = swap_shards(up_back)
    pair_back = jnp.concatenate([gate_back, up_back], axis=1)
    pair_back, attn_peer, two_peer = lax.optimization_barrier((pair_back, attn_peer, two_peer))
    grad_xn_two = jnp.dot(pair_back, w_pair.T, preferred_element_type=jnp.float32)
    back_two, gain_grad_two = pull_two(grad_xn_two)
    grad_resid = out_grad.astype(jnp.float32) + back_two
    resid_low = grad_resid.astype(low_type)
    resid_peer = swap_shards(resid_low)
    grad_attn = jnp.dot(resid_low, w_out.T, preferred_element_type=jnp.float32).astype(low_type)
    grad_groups = grad_attn.reshape(local_rows, KVH, group_size, HD).transpose(1, 0, 2, 3)
    backward_groups = []
    for group in range(KVH):
        grad_group = grad_groups[group]
        backward_groups.append(
            group_backward(
                (
                    query_groups[group],
                    key_groups[group],
                    value_groups[group],
                    grad_group,
                    forward_groups[group][1],
                ),
                allowed,
                score_scale,
            )
        )
    grad_q = jnp.stack([terms[0] for terms in backward_groups], axis=1)
    key_terms = jnp.concatenate([terms[1] for terms in backward_groups], axis=1)
    value_terms = jnp.concatenate([terms[2] for terms in backward_groups], axis=1)
    terms = jnp.concatenate([key_terms, value_terms], axis=1)
    terms, gate_peer = lax.optimization_barrier((terms, gate_peer))
    grad_gate = owned_product(two_mine, two_peer, gate_back, gate_peer).reshape(-1, 128)
    gate_part = scatter_replicas(grad_gate, 1)
    terms_mine = terms[:local_rows] + swap_shards(terms[local_rows:].astype(low_type)).astype(
        jnp.float32
    )
    query_back = rotate(
        grad_q.reshape(local_rows, H, HD), cosine, sine_vals, -1.0
    )
    key_back = rotate(terms_mine[:, :KD].reshape(local_rows, KVH, HD), cosine, sine_vals, -1.0)
    qkv_back = jnp.concatenate(
        [
            query_back.reshape(local_rows, QD).astype(low_type),
            key_back.reshape(local_rows, KD).astype(low_type),
            terms_mine[:, KD:].astype(low_type),
        ],
        axis=1,
    )
    qkv_back, up_peer, hidden_peer, gate_part = lax.optimization_barrier(
        (qkv_back, up_peer, hidden_peer, gate_part)
    )
    grad_up = owned_product(two_mine, two_peer, up_back, up_peer).reshape(-1, 128)
    grad_down = owned_product(hidden_mine, hidden_peer, out_grad, out_peer).reshape(-1, 128)
    qkv_peer = swap_shards(qkv_back)
    grad_xn_one = jnp.dot(qkv_back, w_qkv.T, preferred_element_type=jnp.float32)
    back_one, gain_grad_one = pull_one(grad_xn_one)
    input_grad = grad_resid + back_one
    grad_out = owned_product(attn_mine, attn_peer, resid_low, resid_peer)
    grad_qkv = owned_product(one_mine, one_peer, qkv_back, qkv_peer)
    gain_local = jnp.stack([gain_grad_one, gain_grad_two])
    gain_mine, gain_theirs = split_columns(gain_local, my_shard)
    gain_rows = (gain_mine + swap_shards(gain_theirs)).astype(low_type).reshape(-1)
    gain_rows = jnp.pad(gain_rows, (0, 128 * 128 - gain_rows.shape[0])).reshape(128, 128)
    half_rows = BLOCK * CHUNK_BLOCKS // 2
    key_rows = grad_qkv[:, QD : QD + KD].reshape(-1, 128)
    grad_attn_owned = jnp.concatenate(
        [
            grad_qkv[:, :QD].reshape(-1, 128),
            key_rows,
            gain_rows[:64],
            grad_qkv[:, QD + KD :].reshape(-1, 128),
            grad_out.reshape(-1, 128),
            gain_rows[64:],
        ],
        axis=0,
    )
    gate_sum = gather_halves(scatter_steps(gate_part, 2, replica_count))
    up_sum = gather_halves(scatter_steps(grad_up, 1, replica_count))
    down_sum = gather_halves(scatter_steps(grad_down, 1, replica_count))
    attn_part = scatter_steps(grad_attn_owned, 1, replica_count)
    core = lax.axis_index("dp") % 2
    bit = core.reshape(1).astype(jnp.int32)
    rates = matrix_rates(longest)
    state = [values.reshape(-1, 128) for values in (params, first_moment, second_moment)]
    *updated, mark = update_chunk(state, gate_sum, bit, 1, (rates[4], rates[4]), 0, ())
    attn_part, mark = lax.optimization_barrier((attn_part, mark))
    attn_piece = gather_steps(attn_part, replica_count // 2, 4)
    *updated, mark = update_chunk(state, up_sum, bit, 2, (rates[5], rates[5]), 0, updated)
    attn_piece, mark = lax.optimization_barrier((attn_piece, mark))
    attn_piece = gather_steps(attn_piece, 2, 2)
    attn_sum = (attn_piece, swap_replicas(attn_piece, 1))
    *updated, mark = update_chunk(state, down_sum, bit, 3, (rates[6], rates[6]), 0, updated)
    *updated, mark = update_chunk(state, attn_sum, bit, 0, (rates[0], rates[3]), 5, updated)
    gain_sum = jnp.where(core == 0, attn_sum[0][half_rows:], attn_sum[1][half_rows:])
    gain_owned = gain_sum[:8].reshape(-1)[: 2 * (D // shard_count)]
    gain_owned = gain_owned.reshape(2, -1).astype(jnp.float32)
    owned_grad, new_first, new_second, new_params = [values.reshape(-1) for values in updated]
    new_gain_first, new_gain_second, new_gains = adamw_step(
        norm_gains, gain_owned, gain_first, gain_second, gain_rate, 0.0
    )
    return (
        block_out,
        input_grad,
        owned_grad,
        new_first,
        new_second,
        new_params,
        gain_owned,
        new_gain_first,
        new_gain_second,
        new_gains,
    )


def solution(mesh):
    return jax.shard_map(
        body,
        mesh=mesh,
        in_specs=(
            P(("dp", "cp"), None),
            P(("dp", "cp"), None),
            P("dp", None),
            P("dp", None),
            P("cp"),
            P("cp"),
            P("cp"),
            P(None, "cp"),
            P(None, "cp"),
            P(None, "cp"),
        ),
        out_specs=(
            P(("dp", "cp"), None),
            P(("dp", "cp"), None),
            P("cp"),
            P("cp"),
            P("cp"),
            P("cp"),
            P(None, "cp"),
            P(None, "cp"),
            P(None, "cp"),
            P(None, "cp"),
        ),
        check_vma=False,
    )
```

```python
import jax
import jax.numpy as jnp
from jax import lax
from jax.experimental import pallas as pl
from jax.experimental.pallas import tpu as pltpu
from jax.sharding import PartitionSpec as P

D = 960
H = 15
KVH = 5
HD = 64
FF = 2560
STEP = 10
QD = 960
KD = 320


eps_norm = 1e-05
beta_one = 0.9
beta_two = 0.95
adam_eps = 1e-08
decay_coef = 0.1
rope_base = 10000.0
gain_rate = 1.0
masked_score = -1e30


def matrix_shapes():
    return [(D, QD), (D, KD), (D, KD), (QD, D), (D, FF), (D, FF), (FF, D)]


def matrix_rates(longest):
    plain_rate = 3.0 * D ** (-0.5)
    out_rate = 3.0 * (longest / (6.0 * QD)) ** 0.5
    return [
        plain_rate,
        plain_rate,
        plain_rate,
        out_rate,
        plain_rate,
        plain_rate,
        3.0 * FF ** (-0.5),
    ]


def rms_norm(values, gain_row):
    return (
        values * lax.rsqrt(jnp.mean(values * values, axis=-1, keepdims=True) + eps_norm) * gain_row
    )


def swiglu(gate_act, up_act):
    return jax.nn.silu(gate_act) * up_act


def window_layout(seq_lengths, slot_pos):
    seq_ends = jnp.cumsum(seq_lengths)
    seq_starts = seq_ends - seq_lengths
    segment = jnp.sum((slot_pos[:, None] >= seq_ends[None, :]).astype(jnp.int32), axis=1)
    chosen = segment[:, None] == jnp.arange(seq_lengths.shape[0], dtype=jnp.int32)[None, :]
    position = slot_pos - jnp.sum(jnp.where(chosen, seq_starts[None, :], 0), axis=1)
    return (segment, position)


def rope_tables(position):
    half_dim = HD // 2
    inv_freq = rope_base ** (-(jnp.arange(half_dim, dtype=jnp.float32) * 2.0 / HD))
    angles = position.astype(jnp.float32)[:, None] * inv_freq[None, :]
    return (jnp.cos(angles), jnp.sin(angles))


def rotate(values, cosine, sine_vals, direction):
    half_dim = HD // 2
    first_half = values[..., :half_dim]
    second_half = values[..., half_dim:]
    cos_wide = cosine[:, None, :]
    sin_wide = direction * sine_vals[:, None, :]
    return jnp.concatenate(
        [
            first_half * cos_wide - second_half * sin_wide,
            second_half * cos_wide + first_half * sin_wide,
        ],
        axis=-1,
    )


def group_forward(group_args, allowed, score_scale):
    query_grp, key_grp, value_grp = group_args
    raw_scores = jnp.einsum("qhd,kd->hqk", query_grp, key_grp, preferred_element_type=jnp.float32)
    scores = jnp.where(allowed[None], raw_scores * score_scale, masked_score)
    row_max = jnp.max(scores, axis=-1, keepdims=True)
    exp_scores = jnp.exp(scores - row_max)
    row_total = jnp.sum(exp_scores, axis=-1, keepdims=True)
    probs_low = (exp_scores / row_total).astype(jnp.bfloat16)
    output = jnp.einsum("hqk,kd->qhd", probs_low, value_grp, preferred_element_type=jnp.float32)
    return (output, row_max + jnp.log(row_total))


def group_backward(group_args, allowed, score_scale):
    query_grp, key_grp, value_grp, grad_grp, log_sums = group_args
    raw_scores = jnp.einsum("qhd,kd->hqk", query_grp, key_grp, preferred_element_type=jnp.float32)
    scores = jnp.where(allowed[None], raw_scores * score_scale, masked_score)
    probs = jnp.exp(scores - log_sums)
    probs_low = probs.astype(jnp.bfloat16)
    grad_probs = jnp.einsum("qhd,kd->hqk", grad_grp, value_grp, preferred_element_type=jnp.float32)
    row_dot = jnp.sum(probs * grad_probs, axis=-1, keepdims=True)
    grad_scores = (probs * (grad_probs - row_dot)).astype(jnp.bfloat16)
    grad_query = (
        jnp.einsum("hqk,kd->qhd", grad_scores, key_grp, preferred_element_type=jnp.float32)
        * score_scale
    )
    grad_key = (
        jnp.einsum("hqk,qhd->kd", grad_scores, query_grp, preferred_element_type=jnp.float32)
        * score_scale
    )
    grad_value = jnp.einsum("hqk,qhd->kd", probs_low, grad_grp, preferred_element_type=jnp.float32)
    return (grad_query, grad_key, grad_value)


def adamw_step(weight, gradient, first_old, second_old, step_rates, decay_value):
    first_new = beta_one * first_old + (1.0 - beta_one) * gradient
    second_new = beta_two * second_old + (1.0 - beta_two) * gradient * gradient
    first_hat = first_new / (1.0 - beta_one**STEP)
    second_hat = second_new / (1.0 - beta_two**STEP)
    updated = weight - step_rates * (
        first_hat / (jnp.sqrt(second_hat) + adam_eps) + decay_value * weight
    )
    return (first_new, second_new, updated)


def swap_shards(values):
    return lax.ppermute(values, "cp", [(0, 1), (1, 0)])


def swap_replicas(values, distance):
    return lax.ppermute(
        values, "dp", [(index, index ^ distance) for index in range(lax.axis_size("dp"))]
    )


def in_order(mine, theirs, my_shard, axis):
    return jnp.where(
        my_shard == 0,
        jnp.concatenate([mine, theirs], axis=axis),
        jnp.concatenate([theirs, mine], axis=axis),
    )


def split_columns(values, my_shard):
    half = values.shape[1] // 2
    lower, upper = values[:, :half], values[:, half:]
    return (jnp.where(my_shard == 0, lower, upper), jnp.where(my_shard == 0, upper, lower))


def fetch_quarter(params, columns):
    quarter = lax.axis_index("dp") % 4
    pieces = [
        lax.dynamic_slice_in_dim(
            params, offset + quarter * (rows // 4 * width), rows // 4 * width
        )
        .astype(jnp.bfloat16)
        .reshape(1, rows // 4, width)
        for offset, rows, width in columns
    ]
    return swap_shards(jnp.concatenate(pieces, axis=2))


def own_rows(params, columns):
    offset, rows, width = columns
    return (
        params[offset : offset + rows * width].astype(jnp.bfloat16).reshape(4, rows // 4, width)
    )


def gather_rows(mine, fetched, across):
    quarter = lax.axis_index("dp") % 4
    mine = jnp.concatenate(mine, axis=2)
    whole = jnp.concatenate([mine, mine], axis=0)
    other = (1 - lax.axis_index("cp")) * 4
    for piece, place in (
        (fetched, quarter),
        (across, quarter ^ 2),
        (swap_replicas(fetched, 1), quarter ^ 1),
        (swap_replicas(across, 1), quarter ^ 3),
    ):
        whole = lax.dynamic_update_slice_in_dim(whole, piece, other + place, 0)
    return whole.reshape(-1, whole.shape[2])


def owned_product(left_mine, left_peer, right_mine, right_peer):
    left = jnp.concatenate([left_mine, left_peer], axis=0)
    right = jnp.concatenate([right_mine, right_peer], axis=0)
    return jnp.dot(left.T, right, preferred_element_type=jnp.float32).astype(jnp.bfloat16)


def scatter_replicas(flat, distance):
    bit = (lax.axis_index("dp") // distance) % 2
    halves = flat.reshape(2, flat.shape[0] // 2, flat.shape[1])
    mine = lax.dynamic_index_in_dim(halves, bit, 0, keepdims=False)
    theirs = lax.dynamic_index_in_dim(halves, 1 - bit, 0, keepdims=False)
    received = swap_replicas(theirs, distance)
    return (mine.astype(jnp.float32) + received.astype(jnp.float32)).astype(jnp.bfloat16)


def scatter_steps(flat, distance, limit):
    while distance < limit:
        flat = scatter_replicas(flat, distance)
        distance *= 2
    return flat


def gather_steps(piece, distance, last):
    while distance >= last:
        bit = (lax.axis_index("dp") // distance) % 2
        piece = in_order(piece, swap_replicas(piece, distance), bit, 0)
        distance //= 2
    return piece


def gather_halves(part):
    piece = gather_steps(part, lax.axis_size("dp") // 2, 2)
    return (piece, swap_replicas(piece, 1))


BLOCK = 1200
CHUNK_BLOCKS = 8


def update_kernel(first_rate, last_rate, split, bit_ref, *refs):
    params_ref, first_ref, second_ref, mine_ref, received_ref = refs[:5]
    grad_out, first_out, second_out, params_out, mark_out = refs[-5:]
    mark_out[...] = jnp.zeros_like(mark_out)
    own_half = pl.program_id(0) // (CHUNK_BLOCKS // 2) == bit_ref[0]
    gradient = jnp.where(
        own_half, mine_ref[...].astype(jnp.float32), received_ref[...].astype(jnp.float32)
    )
    rate = jnp.where(pl.program_id(0) < split, first_rate, last_rate)
    grad_out[...] = gradient
    first_out[...], second_out[...], params_out[...] = adamw_step(
        params_ref[...], gradient, first_ref[...], second_ref[...], rate, decay_coef
    )


def update_chunk(state, halves, bit, chunk, rates, split, earlier):
    rows = state[0].shape[0]

    def state_block(i):
        return (chunk * CHUNK_BLOCKS + i, 0)

    spec = pl.BlockSpec((BLOCK, 128), state_block)
    half_spec = pl.BlockSpec((BLOCK, 128), lambda i: (i % (CHUNK_BLOCKS // 2), 0))
    return pl.pallas_call(
        lambda *refs: update_kernel(rates[0], rates[1], split, *refs),
        grid=(CHUNK_BLOCKS,),
        in_specs=[pl.BlockSpec(memory_space=pltpu.SMEM)]
        + [spec] * 3
        + [half_spec] * 2
        + [pl.BlockSpec(memory_space=pl.ANY)] * len(earlier),
        out_specs=[spec] * 4 + [pl.BlockSpec((8, 128), lambda i: (0, 0))],
        out_shape=[jax.ShapeDtypeStruct((rows, 128), jnp.float32)] * 4
        + [jax.ShapeDtypeStruct((8, 128), jnp.float32)],
        input_output_aliases={6 + index: index for index in range(len(earlier))},
        compiler_params=pltpu.CompilerParams(vmem_limit_bytes=40 * 1024 * 1024),
        cost_estimate=pl.CostEstimate(
            flops=20 * BLOCK * CHUNK_BLOCKS * 128,
            bytes_accessed=32 * BLOCK * CHUNK_BLOCKS * 128,
            transcendentals=0,
        ),
    )(bit, *state, *halves, *earlier)


def body(
    tokens,
    out_grad,
    lengths,
    slot_positions,
    params,
    first_moment,
    second_moment,
    norm_gains,
    gain_first,
    gain_second,
):
    low_type = jnp.bfloat16
    shard_count = lax.axis_size("cp")
    replica_count = lax.axis_size("dp")
    local_rows = tokens.shape[0]
    longest = local_rows * shard_count // 2
    group_size = H // KVH
    score_scale = HD ** (-0.5)
    my_shard = lax.axis_index("cp")
    blocks = []
    offset = 0
    for row_count, col_count in matrix_shapes():
        blocks.append((offset, row_count // shard_count, col_count))
        offset += row_count // shard_count * col_count
    gains_low = norm_gains.astype(low_type)
    gain_pair = in_order(gains_low, swap_shards(gains_low), my_shard, 1)
    fetched = [
        fetch_quarter(params, columns)
        for columns in (blocks[:3], blocks[3:4], blocks[4:6], blocks[6:])
    ]
    own_qkv = [own_rows(params, columns) for columns in blocks[:3]]
    own_out = own_rows(params, blocks[3])
    held, fetched[0], fetched[1], fetched[2] = lax.optimization_barrier(
        (params, fetched[0], fetched[1], fetched[2])
    )
    across = [swap_replicas(piece, 2) for piece in fetched]
    own_gate = own_rows(held, blocks[4])
    held, across[0], across[1], across[2] = lax.optimization_barrier(
        (held, across[0], across[1], across[2])
    )
    own_up = own_rows(held, blocks[5])
    own_down = own_rows(held, blocks[6])
    w_qkv = gather_rows(own_qkv, fetched[0], across[0])
    w_out = gather_rows([own_out], fetched[1], across[1])
    w_pair = gather_rows([own_gate, own_up], fetched[2], across[2])
    w_down = gather_rows([own_down], fetched[3], across[3])

    out_peer = swap_shards(out_grad)
    segment_all, position_all = window_layout(lengths[0], slot_positions[0])

    def shard_rows(values, shard):
        return lax.dynamic_slice_in_dim(values, shard * local_rows, local_rows)

    segment_mine = shard_rows(segment_all, my_shard)
    position_mine = shard_rows(position_all, my_shard)
    segment_keys = jnp.concatenate([segment_mine, shard_rows(segment_all, 1 - my_shard)])
    position_keys = jnp.concatenate([position_mine, shard_rows(position_all, 1 - my_shard)])
    allowed = (segment_mine[:, None] == segment_keys[None, :]) & (
        position_keys[None, :] <= position_mine[:, None]
    )
    cosine, sine_vals = rope_tables(position_mine)
    inputs = tokens.astype(jnp.float32)
    normed_one, pull_one = jax.vjp(rms_norm, inputs, gain_pair[0].astype(jnp.float32))
    xn_one = normed_one.astype(low_type)
    one_mine, one_theirs = split_columns(xn_one, my_shard)
    one_peer = swap_shards(one_theirs)
    qkv_pre = jnp.dot(xn_one, w_qkv, preferred_element_type=jnp.float32)
    query_pre = qkv_pre[:, :QD]
    key_pre = qkv_pre[:, QD : QD + KD]
    value_low = qkv_pre[:, QD + KD :].astype(low_type)
    query_rot = rotate(query_pre.reshape(local_rows, H, HD), cosine, sine_vals, 1.0).astype(
        low_type
    )
    key_rot = rotate(key_pre.reshape(local_rows, KVH, HD), cosine, sine_vals, 1.0).astype(low_type)
    key_value = jnp.concatenate([key_rot.reshape(local_rows, KD), value_low], axis=1)
    key_value = jnp.concatenate([key_value, swap_shards(key_value)], axis=0)
    key_groups = key_value[:, :KD].reshape(-1, KVH, HD).transpose(1, 0, 2)
    value_groups = key_value[:, KD:].reshape(-1, KVH, HD).transpose(1, 0, 2)
    query_groups = query_rot.reshape(local_rows, KVH, group_size, HD).transpose(1, 0, 2, 3)
    forward_groups = [
        group_forward(
            (query_groups[group], key_groups[group], value_groups[group]), allowed, score_scale
        )
        for group in range(KVH)
    ]
    attn_low = jnp.concatenate(
        [attended.reshape(local_rows, -1).astype(low_type) for attended, _ in forward_groups],
        axis=1,
    )
    attn_low, one_peer, out_peer = lax.optimization_barrier((attn_low, one_peer, out_peer))
    attn_mine, attn_theirs = split_columns(attn_low, my_shard)
    attn_peer = swap_shards(attn_theirs)
    resid_one = inputs + jnp.dot(attn_low, w_out, preferred_element_type=jnp.float32)
    normed_two, pull_two = jax.vjp(rms_norm, resid_one, gain_pair[1].astype(jnp.float32))
    xn_two = normed_two.astype(low_type)
    two_mine, two_theirs = split_columns(xn_two, my_shard)
    two_peer = swap_shards(two_theirs)
    pair_act = jnp.dot(xn_two, w_pair, preferred_element_type=jnp.float32)
    gate_act = pair_act[:, :FF]
    up_act = pair_act[:, FF:]
    hidden_act, pull_act = jax.vjp(swiglu, gate_act, up_act)
    hidden_low = hidden_act.astype(low_type)
    hidden_mine, hidden_theirs = split_columns(hidden_low, my_shard)
    hidden_peer = swap_shards(hidden_theirs)
    block_out = resid_one + jnp.dot(hidden_low, w_down, preferred_element_type=jnp.float32)
    grad_hidden = jnp.dot(out_grad, w_down.T, preferred_element_type=jnp.float32)
    grad_gate_act, grad_up_act = pull_act(grad_hidden)
    gate_back = grad_gate_act.astype(low_type)
    up_back = grad_up_act.astype(low_type)
    gate_peer = swap_shards(gate_back)
    up_peer = swap_shards(up_back)
    pair_back = jnp.concatenate([gate_back, up_back], axis=1)
    pair_back, attn_peer, two_peer = lax.optimization_barrier((pair_back, attn_peer, two_peer))
    grad_xn_two = jnp.dot(pair_back, w_pair.T, preferred_element_type=jnp.float32)
    back_two, gain_grad_two = pull_two(grad_xn_two)
    grad_resid = out_grad.astype(jnp.float32) + back_two
    resid_low = grad_resid.astype(low_type)
    resid_peer = swap_shards(resid_low)
    grad_attn = jnp.dot(resid_low, w_out.T, preferred_element_type=jnp.float32).astype(low_type)
    grad_groups = grad_attn.reshape(local_rows, KVH, group_size, HD).transpose(1, 0, 2, 3)
    backward_groups = []
    for group in range(KVH):
        grad_group = grad_groups[group]
        backward_groups.append(
            group_backward(
                (
                    query_groups[group],
                    key_groups[group],
                    value_groups[group],
                    grad_group,
                    forward_groups[group][1],
                ),
                allowed,
                score_scale,
            )
        )
    grad_q = jnp.stack([terms[0] for terms in backward_groups], axis=1)
    key_terms = jnp.concatenate([terms[1] for terms in backward_groups], axis=1)
    value_terms = jnp.concatenate([terms[2] for terms in backward_groups], axis=1)
    terms = jnp.concatenate([key_terms, value_terms], axis=1)
    terms, gate_peer = lax.optimization_barrier((terms, gate_peer))
    grad_gate = owned_product(two_mine, two_peer, gate_back, gate_peer).reshape(-1, 128)
    gate_part = scatter_replicas(grad_gate, 1)
    terms_mine = terms[:local_rows] + swap_shards(terms[local_rows:].astype(low_type)).astype(
        jnp.float32
    )
    query_back = rotate(
        grad_q.reshape(local_rows, H, HD), cosine, sine_vals, -1.0
    )
    key_back = rotate(terms_mine[:, :KD].reshape(local_rows, KVH, HD), cosine, sine_vals, -1.0)
    qkv_back = jnp.concatenate(
        [
            query_back.reshape(local_rows, QD).astype(low_type),
            key_back.reshape(local_rows, KD).astype(low_type),
            terms_mine[:, KD:].astype(low_type),
        ],
        axis=1,
    )
    qkv_back, up_peer, hidden_peer, gate_part = lax.optimization_barrier(
        (qkv_back, up_peer, hidden_peer, gate_part)
    )
    grad_up = owned_product(two_mine, two_peer, up_back, up_peer).reshape(-1, 128)
    grad_down = owned_product(hidden_mine, hidden_peer, out_grad, out_peer).reshape(-1, 128)
    qkv_peer = swap_shards(qkv_back)
    grad_xn_one = jnp.dot(qkv_back, w_qkv.T, preferred_element_type=jnp.float32)
    back_one, gain_grad_one = pull_one(grad_xn_one)
    input_grad = grad_resid + back_one
    grad_out = owned_product(attn_mine, attn_peer, resid_low, resid_peer)
    grad_qkv = owned_product(one_mine, one_peer, qkv_back, qkv_peer)
    gain_local = jnp.stack([gain_grad_one, gain_grad_two])
    gain_mine, gain_theirs = split_columns(gain_local, my_shard)
    gain_rows = (gain_mine + swap_shards(gain_theirs)).astype(low_type).reshape(-1)
    gain_rows = jnp.pad(gain_rows, (0, 128 * 128 - gain_rows.shape[0])).reshape(128, 128)
    half_rows = BLOCK * CHUNK_BLOCKS // 2
    key_rows = grad_qkv[:, QD : QD + KD].reshape(-1, 128)
    grad_attn_owned = jnp.concatenate(
        [
            grad_qkv[:, :QD].reshape(-1, 128),
            key_rows,
            gain_rows[:64],
            grad_qkv[:, QD + KD :].reshape(-1, 128),
            grad_out.reshape(-1, 128),
            gain_rows[64:],
        ],
        axis=0,
    )
    gate_sum = gather_halves(scatter_steps(gate_part, 2, replica_count))
    up_sum = gather_halves(scatter_steps(grad_up, 1, replica_count))
    down_sum = gather_halves(scatter_steps(grad_down, 1, replica_count))
    attn_part = scatter_steps(grad_attn_owned, 1, replica_count)
    core = lax.axis_index("dp") % 2
    bit = core.reshape(1).astype(jnp.int32)
    rates = matrix_rates(longest)
    state = [values.reshape(-1, 128) for values in (params, first_moment, second_moment)]
    *updated, mark = update_chunk(state, gate_sum, bit, 1, (rates[4], rates[4]), 0, ())
    attn_part = attn_part + mark[:1].astype(low_type)
    attn_piece = gather_steps(attn_part, replica_count // 2, 4)
    *updated, mark = update_chunk(state, up_sum, bit, 2, (rates[5], rates[5]), 0, updated)
    attn_piece = attn_piece + mark[:1].astype(low_type)
    attn_piece = gather_steps(attn_piece, 2, 2)
    attn_sum = (attn_piece, swap_replicas(attn_piece, 1))
    *updated, mark = update_chunk(state, down_sum, bit, 3, (rates[6], rates[6]), 0, updated)
    *updated, mark = update_chunk(state, attn_sum, bit, 0, (rates[0], rates[3]), 5, updated)
    gain_sum = jnp.where(core == 0, attn_sum[0][half_rows:], attn_sum[1][half_rows:])
    gain_owned = gain_sum[:8].reshape(-1)[: 2 * (D // shard_count)]
    gain_owned = gain_owned.reshape(2, -1).astype(jnp.float32)
    owned_grad, new_first, new_second, new_params = [values.reshape(-1) for values in updated]
    new_gain_first, new_gain_second, new_gains = adamw_step(
        norm_gains, gain_owned, gain_first, gain_second, gain_rate, 0.0
    )
    return (
        block_out,
        input_grad,
        owned_grad,
        new_first,
        new_second,
        new_params,
        gain_owned,
        new_gain_first,
        new_gain_second,
        new_gains,
    )


def solution(mesh):
    return jax.shard_map(
        body,
        mesh=mesh,
        in_specs=(
            P(("dp", "cp"), None),
            P(("dp", "cp"), None),
            P("dp", None),
            P("dp", None),
            P("cp"),
            P("cp"),
            P("cp"),
            P(None, "cp"),
            P(None, "cp"),
            P(None, "cp"),
        ),
        out_specs=(
            P(("dp", "cp"), None),
            P(("dp", "cp"), None),
            P("cp"),
            P("cp"),
            P("cp"),
            P("cp"),
            P(None, "cp"),
            P(None, "cp"),
            P(None, "cp"),
            P(None, "cp"),
        ),
        check_vma=False,
    )
```
